32 devices in a mesh: fsdp: 8 (over y, x, core), tp: 4 (over z).
Axes of the slice: x: 2, y: 2, z: 4, core: 2. Of those that a mesh axis runs over, the one named last changes fastest.
Arguments:
- tokens: bfloat16 [512, 5120], P(('fsdp', 'tp')), may hold values from -6 to 6
- tile_values: bfloat16 [128, 840, 128], P('fsdp', 'tp'), may hold values from -0.15625 to 0.15625
- tile_row: int32 [4, 210], P('tp'), may hold values from 0 to 39, as said below
- tile_col: int32 [4, 210], P('tp'), may hold values from 0 to 20, as said below
- grad_act: bfloat16 [512, 10752], P('fsdp', 'tp'), may hold values from -6 to 6
Outputs:
- act: bfloat16 [512, 10752], P('fsdp', 'tp')
- grad_tokens: bfloat16 [512, 5120], P(('fsdp', 'tp'))
- grad_tiles: float32 [128, 840, 128], P('fsdp', 'tp')
The draws below stay inside these ranges and needn't reach their ends.
Inputs may be any that keep to these rules, and one draw needn't show every extreme that they name: Within each of the 4 shards the pairs (tile_row, tile_col) of its 210 slots are distinct; every shard has one slot at tile row 39 and tile column 20. `tile_col`: the pairs are those of tile_row.
All inputs are finite; a program needn't handle non-finite values.
Results may differ from the reference program's by a relative error of at most 0.0095.
Values may be sent and summed in bfloat16 or wider, within the bound.
No kernel may reach another device: no remote copies, remote signals or barrier semaphores. Data moves between devices by JAX's collectives and lax.ppermute only.
A program may use at most 128 MiB of HBM per device.

```python
import math
import jax
import jax.numpy as jnp
from jax import lax

TILE = 128
D = 5120
FF = 10752
ROW_TILES = 40
COL_TILES = 21
TILES_SHARD = 210
TOKENS = 512
N_TP = 4


def shard_places(shard_key):
    total = ROW_TILES * COL_TILES
    first_key, second_key = jax.random.split(shard_key)
    others = jax.random.permutation(first_key, total - 1)[:TILES_SHARD - 1].astype(jnp.int32)
    places = jnp.concatenate([others, jnp.full((1,), total - 1, jnp.int32)])
    order = jax.random.permutation(second_key, TILES_SHARD)
    return places[order]


def tile_places(key):
    shard_keys = jax.random.split(key, N_TP)
    return jax.vmap(shard_places)(shard_keys)


def draw_tile_row(key, part):
    places = tile_places(key)
    return (places // COL_TILES).astype(jnp.int32)


def draw_tile_col(key, part):
    places = tile_places(key)
    return (places % COL_TILES).astype(jnp.int32)


def block_scale(own_key, dims, pieces, least, top_value):
    level = 1.0
    for dim, shards_of in pieces:
        draws = jax.random.uniform(jax.random.fold_in(jax.random.fold_in(own_key, 6), dim), (shards_of,), jnp.float32, least / len(pieces), top_value / len(pieces))
        level = level * jnp.repeat(jnp.exp(draws), dims[dim] // shards_of).reshape((-1,) + (1,) * (len(dims) - 1 - dim))
    return level


def normal_values(key, shape, scale, reach, shards=(), kind=jnp.bfloat16):
    values = scale * jax.random.normal(key, shape, jnp.float32)
    if shards:
        values = values * block_scale(key, shape, shards, -0.22, 0.18)
    return jnp.clip(values, -reach, reach).astype(kind)


def setup_inputs(seed: int = 0) -> dict:
    streams_of = jax.random.split(jax.random.key(seed), 6)
    return {
        "tokens": normal_values(streams_of[0], (TOKENS, D), 1.0, 6.0, ((0, 32),)),
        "tile_values": normal_values(streams_of[1], (TILE, N_TP * TILES_SHARD, TILE), (D // 4) ** -0.5, 0.15625, ((0, 8), (1, 4))),
        "tile_row": draw_tile_row(jax.random.fold_in(streams_of[5], 71), 0),
        "tile_col": draw_tile_col(jax.random.fold_in(streams_of[5], 71), 0),
        "grad_act": normal_values(streams_of[4], (TOKENS, FF), 1.0, 6.0, ((0, 8), (1, 4))),
    }


SQRT_TWO_PI = 0.7978845608028654
CUBIC_COEF = 0.044715

def gelu_pair(pre_act):
    gelu_inner = SQRT_TWO_PI * (pre_act + CUBIC_COEF * pre_act * pre_act * pre_act)
    tanh_inner = jnp.tanh(gelu_inner)
    act_value = 0.5 * pre_act * (1.0 + tanh_inner)
    act_slope = 0.5 * (1.0 + tanh_inner) + 0.5 * pre_act * (1.0 - tanh_inner * tanh_inner) * SQRT_TWO_PI * (1.0 + 3.0 * CUBIC_COEF * pre_act * pre_act)
    return (act_value, act_slope)

def reference(tokens, tile_values, tile_row, tile_col, grad_act):
    highest = lax.Precision.HIGHEST
    blocks = tokens.reshape(TOKENS, ROW_TILES, TILE)
    values = jnp.transpose(tile_values.reshape(TILE, N_TP, TILES_SHARD, TILE), (1, 0, 2, 3))
    grad_parts = jnp.transpose(grad_act.reshape(TOKENS, N_TP, COL_TILES, TILE), (1, 0, 2, 3))
    grad_scale = 1.0 / math.sqrt(TOKENS)

    def per_shard(carried, inputs):
        tile_block, row_index, col_index, grad_part = inputs
        row_onehot = (row_index[:, None] == jnp.arange(ROW_TILES, dtype=jnp.int32)[None, :]).astype(jnp.float32)
        col_onehot = (col_index[:, None] == jnp.arange(COL_TILES, dtype=jnp.int32)[None, :]).astype(jnp.float32)
        tile_wide = tile_block.astype(jnp.float32)
        chosen = jnp.take(blocks, row_index, axis=1).astype(jnp.float32)
        product = jnp.einsum('tnk,knj->tnj', chosen, tile_wide, precision=highest)
        hidden = jnp.einsum('tnj,nc->tcj', product, col_onehot, precision=highest)
        act_value, act_slope = gelu_pair(hidden)
        act_part = act_value.astype(jnp.bfloat16)
        hidden_grad = (grad_part.astype(jnp.float32) * act_slope).astype(jnp.bfloat16)
        grad_selected = jnp.take(hidden_grad, col_index, axis=1).astype(jnp.float32)
        back_product = jnp.einsum('tnj,knj->tnk', grad_selected, tile_wide, precision=highest)
        partial_value = jnp.einsum('tnk,nq->tqk', back_product, row_onehot, precision=highest).astype(jnp.bfloat16)
        carried = carried + partial_value.astype(jnp.float32)
        tile_grad = jnp.einsum('tnk,tnj->knj', chosen, grad_selected, precision=highest) * grad_scale
        return (carried, (act_part, tile_grad))
    summed_rows, (act_stack, grad_stack) = lax.scan(per_shard, jnp.zeros((TOKENS, ROW_TILES, TILE), jnp.float32), (values, tile_row, tile_col, grad_parts))
    act = jnp.transpose(act_stack, (1, 0, 2, 3)).reshape(TOKENS, FF)
    grad_tokens = summed_rows.reshape(TOKENS, D).astype(jnp.bfloat16)
    grad_tiles = jnp.transpose(grad_stack, (1, 0, 2, 3)).reshape(TILE, N_TP * TILES_SHARD, TILE)
    return (act, grad_tokens, grad_tiles)
```

```python
import functools
import math

import jax
import jax.numpy as jnp
from jax import lax
from jax.experimental import pallas as pl
from jax.experimental.pallas import tpu as pltpu
from jax.sharding import PartitionSpec as P

SQRT_TWO_PI = 0.7978845608028654
CUBIC_COEF = 0.044715
BF16 = jnp.bfloat16
F32 = jnp.float32
VMEM = pltpu.VMEM
SMEM = pltpu.SMEM
MIB = 1 << 20


def gelu_pair(pre_act):
    gelu_inner = SQRT_TWO_PI * (pre_act + CUBIC_COEF * pre_act * pre_act * pre_act)
    tanh_inner = jnp.tanh(gelu_inner)
    act_value = 0.5 * pre_act * (1.0 + tanh_inner)
    act_slope = 0.5 * (1.0 + tanh_inner) + 0.5 * pre_act * (
        1.0 - tanh_inner * tanh_inner
    ) * SQRT_TWO_PI * (1.0 + 3.0 * CUBIC_COEF * pre_act * pre_act)
    return (act_value, act_slope)


def spec(space=VMEM):
    return pl.BlockSpec(memory_space=space)


def lane_regroup(chips, tile_width):
    size = chips * tile_width
    part = tile_width // chips
    column = lax.broadcasted_iota(jnp.int32, (1, size), 1)
    chip = column // tile_width
    inner = column % tile_width
    source = (inner // part) * tile_width + chip * part + inner % part
    row = lax.broadcasted_iota(jnp.int32, (size, size), 0)
    return jnp.where(row == source, 1.0, 0.0).astype(BF16)


def split_kernel(chips, tile_width, chip_ref, tokens_ref, out_ref):
    size = chips * tile_width
    onehot = lane_regroup(chips, tile_width)
    me = chip_ref[0]
    for group in range(tokens_ref.shape[1] // size):
        picked = jnp.dot(
            tokens_ref[:, group * size : (group + 1) * size], onehot, preferred_element_type=F32
        ).astype(BF16)
        for chip in range(chips):
            out_ref[me ^ chip, :, group * tile_width : (group + 1) * tile_width] = picked[
                :, chip * tile_width : (chip + 1) * tile_width
            ]


def join_kernel(chips, tile_width, chip_ref, *refs):
    *part_refs, out_ref, held = refs
    size = chips * tile_width
    onehot = lane_regroup(chips, tile_width)
    me = chip_ref[0]
    for step in range(chips):
        held[me ^ step] = part_refs[step][...]
    for group in range(out_ref.shape[1] // size):
        lanes = jnp.concatenate(
            [held[chip, :, group * tile_width : (group + 1) * tile_width] for chip in range(chips)],
            axis=1,
        )
        out_ref[:, group * size : (group + 1) * size] = lax.dot_general(
            lanes, onehot, (((1,), (1,)), ((), ())), preferred_element_type=F32
        ).astype(BF16)


def weight_kernel(core_ref, row_ref, col_ref, own_ref, other_ref, out_ref):
    slots, rows, width = own_ref.shape
    core = core_ref[0]
    out_ref[...] = jnp.zeros_like(out_ref)

    def place(slot, carry):
        top = row_ref[0, slot] * (2 * rows)
        left = pl.multiple_of(col_ref[0, slot] * width, width)
        mine = pl.multiple_of(top + core * rows, rows)
        theirs = pl.multiple_of(top + (1 - core) * rows, rows)
        out_ref[pl.ds(mine, rows), pl.ds(left, width)] = own_ref[slot]
        out_ref[pl.ds(theirs, rows), pl.ds(left, width)] = other_ref[slot]
        return carry

    lax.fori_loop(0, slots, place, 0, unroll=6)


def hidden_kernel(chips, count, *refs):
    x_refs = refs[:count]
    w_ref = refs[count]
    out_refs = refs[count + 1 :]
    rows = x_refs[0].shape[1]
    lhs = jnp.concatenate(
        [x_refs[j][step] for step in range(chips) for j in range(count)], axis=0
    )
    result = jnp.dot(lhs, w_ref[...], preferred_element_type=F32)
    block = rows * count
    for step in range(chips):
        out_refs[step][...] = result[step * block : (step + 1) * block].astype(out_refs[step].dtype)


def back_kernel(chips, count, rows, *refs):
    g_refs = refs[:chips]
    w_ref = refs[chips]
    out_refs = refs[chips + 1 :]
    lhs = jnp.concatenate(
        [g_refs[step][j * rows : (j + 1) * rows] for j in range(count) for step in range(chips)],
        axis=0,
    )
    result = lax.dot_general(lhs, w_ref[...], (((1,), (1,)), ((), ())), preferred_element_type=F32)
    block = rows * chips
    for j in range(count):
        out_refs[j][...] = result[j * block : (j + 1) * block].astype(out_refs[j].dtype)


def tile_grad_kernel(chips, plan, rows, core_ref, row_ref, col_ref, *refs):
    zs = sum(len(chunk) for chunk in plan)
    x_refs = refs[:zs]
    g_refs = refs[zs : zs + chips * len(plan)]
    mine_ref, theirs_ref, x_all, g_all, dense = refs[zs + chips * len(plan) :]
    slots, tile_rows, width = mine_ref.shape
    core = core_ref[0]
    at = 0
    for index, chunk in enumerate(plan):
        for place, j in enumerate(chunk):
            for step in range(chips):
                x_all[at : at + rows] = x_refs[j][step]
                g_all[at : at + rows] = g_refs[index * chips + step][
                    place * rows : (place + 1) * rows
                ]
                at += rows
    x_t = x_all[...].T
    columns = dense.shape[1]
    step_width = columns // 3 if columns % (3 * width) == 0 else width
    for left in range(0, columns, step_width):
        dense[:, left : left + step_width] = jnp.dot(
            x_t, g_all[:, left : left + step_width], preferred_element_type=F32
        )

    def place_tile(slot, carry):
        top = row_ref[0, slot] * (2 * tile_rows)
        left = pl.multiple_of(col_ref[0, slot] * width, width)
        mine = pl.multiple_of(top + core * tile_rows, tile_rows)
        theirs = pl.multiple_of(top + (1 - core) * tile_rows, tile_rows)
        mine_ref[slot] = dense[pl.ds(mine, tile_rows), pl.ds(left, width)]
        theirs_ref[slot] = dense[pl.ds(theirs, tile_rows), pl.ds(left, width)]
        return carry

    lax.fori_loop(0, slots, place_tile, 0, unroll=6)


def params(limit):
    return pltpu.CompilerParams(vmem_limit_bytes=limit * MIB)


def cost(flops, bytes_accessed):
    return pl.CostEstimate(flops=flops, bytes_accessed=bytes_accessed, transcendentals=0)


def local(tokens, tile_values, tile_row, tile_col, grad_act):
    fsdp = lax.axis_size("fsdp")
    n_tp = lax.axis_size("tp")
    chips = fsdp // 2
    rows, width = tokens.shape
    tile_rows, slots, tile_width = tile_values.shape
    row_tiles = width // tile_width
    columns = grad_act.shape[1]
    col_tiles = columns // tile_width
    depth = row_tiles * 2 * tile_rows
    total_tokens = rows * fsdp * n_tp
    grad_scale = 1.0 / math.sqrt(total_tokens)
    place = lax.axis_index("fsdp")
    chip = place // 2
    core = place % 2
    z = lax.axis_index("tp")
    fast = tile_rows % 16 == 0 and rows % 16 == 0 and row_tiles % chips == 0
    plan = [tuple(range(n_tp))]

    def to_core(value):
        return lax.ppermute(value, "fsdp", [(f, f ^ 1) for f in range(fsdp)])

    def to_chip(value, step):
        return lax.ppermute(value, "fsdp", [(f, f ^ (2 * step)) for f in range(fsdp)])

    def to_z(value, step):
        return lax.ppermute(value, "tp", [(i, (i + step) % n_tp) for i in range(n_tp)])

    chip_index = chip.astype(jnp.int32).reshape(1)
    core_index = core.astype(jnp.int32).reshape(1)
    own_tiles = jnp.transpose(tile_values, (1, 0, 2))
    other_tiles = to_core(own_tiles)

    if fast:
        split = pl.pallas_call(
            functools.partial(split_kernel, chips, tile_width),
            out_shape=jax.ShapeDtypeStruct((chips, rows, width // chips), BF16),
            in_specs=[spec(SMEM), spec()],
            out_specs=spec(),
            compiler_params=params(16),
        )(chip_index, tokens)
    else:
        split = jnp.transpose(
            tokens.reshape(rows, row_tiles, chips, tile_width // chips), (2, 0, 1, 3)
        ).reshape(chips, rows, depth)
        split = jnp.take(split, jnp.arange(chips) ^ chip, axis=0)
    pieces = [split[0]] + [to_chip(split[step], step) for step in range(1, chips)]
    x_own = jnp.stack(pieces)
    x_parts = [x_own] + [to_z(x_own, j) for j in range(1, n_tp)]

    if fast:
        weight = pl.pallas_call(
            weight_kernel,
            out_shape=jax.ShapeDtypeStruct((depth, columns), BF16),
            in_specs=[spec(SMEM), spec(SMEM), spec(SMEM), spec(), spec()],
            out_specs=spec(),
            compiler_params=params(24),
            cost_estimate=cost(0, 2 * 2 * depth * columns),
        )(core_index, tile_row, tile_col, own_tiles, other_tiles)
    else:
        both = jnp.where(
            core == 0,
            jnp.concatenate([own_tiles, other_tiles], axis=1),
            jnp.concatenate([other_tiles, own_tiles], axis=1),
        )
        flat = tile_row[0] * col_tiles + tile_col[0]
        weight = jnp.zeros((row_tiles * col_tiles, 2 * tile_rows, tile_width), BF16)
        weight = weight.at[flat].set(both, unique_indices=True)
        weight = jnp.transpose(
            weight.reshape(row_tiles, col_tiles, 2 * tile_rows, tile_width), (0, 2, 1, 3)
        ).reshape(depth, columns)

    acts = [None] * n_tp
    grad_chunks = []
    totals = [None] * n_tp
    for chunk in plan:
        count = len(chunk)
        block = rows * count
        chunk_x = [x_parts[j] for j in chunk]
        if fast:
            hidden_parts = pl.pallas_call(
                functools.partial(hidden_kernel, chips, count),
                out_shape=[jax.ShapeDtypeStruct((block, columns), F32)]
                + [jax.ShapeDtypeStruct((block, columns), BF16)] * (chips - 1),
                in_specs=[spec()] * (count + 1),
                out_specs=[spec()] * chips,
                compiler_params=params(32),
                cost_estimate=cost(2 * chips * block * depth * columns, 2 * depth * columns),
            )(*chunk_x, weight)
        else:
            joined = jnp.concatenate(chunk_x, axis=1).reshape(chips * block, depth)
            product = jnp.dot(joined, weight, preferred_element_type=F32)
            product = product.reshape(chips, block, columns)
            hidden_parts = [product[0]] + [
                product[step].astype(BF16) for step in range(1, chips)
            ]
        hidden = hidden_parts[0]
        for step in range(1, chips):
            hidden = hidden + to_chip(hidden_parts[step], step).astype(F32)
        act_value, act_slope = gelu_pair(hidden)
        act_value = act_value.astype(BF16)
        cotangent = jnp.concatenate(
            [
                lax.dynamic_slice_in_dim(grad_act, ((z - j) % n_tp) * rows, rows, axis=0)
                for j in chunk
            ],
            axis=0,
        )
        hidden_grad = (cotangent.astype(F32) * act_slope).astype(BF16)
        for at, j in enumerate(chunk):
            acts[j] = act_value[at * rows : (at + 1) * rows]
        grads = [hidden_grad] + [to_chip(hidden_grad, step) for step in range(1, chips)]
        grad_chunks.append(grads)
        if fast:
            backs = pl.pallas_call(
                functools.partial(back_kernel, chips, count, rows),
                out_shape=[
                    jax.ShapeDtypeStruct((chips * rows, depth), F32 if j == 0 else BF16)
                    for j in chunk
                ],
                in_specs=[spec()] * (chips + 1),
                out_specs=[spec()] * count,
                compiler_params=params(32),
                cost_estimate=cost(2 * chips * block * depth * columns, 2 * depth * columns),
            )(*grads, weight)
        else:
            joined = jnp.stack(grads).reshape(chips, count, rows, columns)
            product = jnp.einsum(
                "sjrc,kc->jsrk", joined, weight, preferred_element_type=F32
            ).reshape(count, chips * rows, depth)
            backs = [
                product[at] if j == 0 else product[at].astype(BF16)
                for at, j in enumerate(chunk)
            ]
        for at, j in enumerate(chunk):
            totals[j] = backs[at]

    total = totals[0]
    for j in range(1, n_tp):
        total = total + to_z(totals[j], n_tp - j).astype(F32)
    total = total.astype(BF16).reshape(chips, rows, depth)
    parts = [total[0]] + [to_chip(total[step], step) for step in range(1, chips)]

    if fast:
        flat_grads = [grad for grads in grad_chunks for grad in grads]
        mine, theirs = pl.pallas_call(
            functools.partial(tile_grad_kernel, chips, plan, rows),
            out_shape=[jax.ShapeDtypeStruct((slots, tile_rows, tile_width), F32)] * 2,
            in_specs=[spec(SMEM)] * 3 + [spec()] * (n_tp + len(flat_grads)),
            out_specs=[spec()] * 2,
            scratch_shapes=[
                pltpu.VMEM((chips * n_tp * rows, depth), BF16),
                pltpu.VMEM((chips * n_tp * rows, columns), BF16),
                pltpu.VMEM((depth, columns), F32),
            ],
            compiler_params=params(40),
            cost_estimate=cost(
                2 * chips * n_tp * rows * depth * columns, 4 * depth * columns
            ),
        )(core_index, tile_row, tile_col, *x_parts, *flat_grads)
        grad_tokens = pl.pallas_call(
            functools.partial(join_kernel, chips, tile_width),
            out_shape=jax.ShapeDtypeStruct((rows, width), BF16),
            in_specs=[spec(SMEM)] + [spec()] * chips,
            out_specs=spec(),
            scratch_shapes=[pltpu.VMEM((chips, rows, depth), BF16)],
            compiler_params=params(16),
        )(chip_index, *parts)
    else:
        x_all = jnp.concatenate(x_parts, axis=1).reshape(-1, depth)
        g_all = jnp.concatenate(
            [jnp.stack(grads) for grads in grad_chunks], axis=1
        ).reshape(-1, columns)
        dense = jnp.einsum("tk,tn->kn", x_all, g_all, preferred_element_type=F32)
        dense = jnp.transpose(
            dense.reshape(row_tiles, 2, tile_rows, col_tiles, tile_width), (1, 0, 3, 2, 4)
        ).reshape(2, row_tiles * col_tiles, tile_rows, tile_width)
        picked = jnp.take(dense, tile_row[0] * col_tiles + tile_col[0], axis=1)
        mine = jnp.where(core == 0, picked[0], picked[1])
        theirs = jnp.where(core == 0, picked[1], picked[0])
        joined = jnp.take(jnp.stack(parts), jnp.arange(chips) ^ chip, axis=0)
        grad_tokens = jnp.transpose(
            joined.reshape(chips, rows, row_tiles, tile_width // chips), (1, 2, 0, 3)
        ).reshape(rows, width)
    grad_tiles = jnp.transpose((mine + to_core(theirs)) * grad_scale, (1, 0, 2))

    act = jnp.zeros((n_tp * rows, columns), BF16)
    for j in range(n_tp):
        act = lax.dynamic_update_slice_in_dim(act, acts[j], ((z - j) % n_tp) * rows, axis=0)
    return (act, grad_tokens, grad_tiles)


def solution(mesh):
    in_specs = (
        P(("fsdp", "tp"), None),
        P("fsdp", "tp", None),
        P("tp", None),
        P("tp", None),
        P("fsdp", "tp"),
    )
    out_specs = (P("fsdp", "tp"), P(("fsdp", "tp"), None), P("fsdp", "tp", None))
    return jax.shard_map(local, mesh=mesh, in_specs=in_specs, out_specs=out_specs, check_vma=False)
```

```python
import functools
import math

import jax
import jax.numpy as jnp
from jax import lax
from jax.experimental import pallas as pl
from jax.experimental.pallas import tpu as pltpu
from jax.sharding import PartitionSpec as P

SQRT_TWO_PI = 0.7978845608028654
CUBIC_COEF = 0.044715
BF16 = jnp.bfloat16
F32 = jnp.float32
VMEM = pltpu.VMEM
SMEM = pltpu.SMEM
MIB = 1 << 20


def gelu_pair(pre_act):
    gelu_inner = SQRT_TWO_PI * (pre_act + CUBIC_COEF * pre_act * pre_act * pre_act)
    tanh_inner = jnp.tanh(gelu_inner)
    act_value = 0.5 * pre_act * (1.0 + tanh_inner)
    act_slope = 0.5 * (1.0 + tanh_inner) + 0.5 * pre_act * (
        1.0 - tanh_inner * tanh_inner
    ) * SQRT_TWO_PI * (1.0 + 3.0 * CUBIC_COEF * pre_act * pre_act)
    return (act_value, act_slope)


def spec(space=VMEM):
    return pl.BlockSpec(memory_space=space)


def lane_regroup(chips, tile_width):
    size = chips * tile_width
    part = tile_width // chips
    column = lax.broadcasted_iota(jnp.int32, (1, size), 1)
    chip = column // tile_width
    inner = column % tile_width
    source = (inner // part) * tile_width + chip * part + inner % part
    row = lax.broadcasted_iota(jnp.int32, (size, size), 0)
    return jnp.where(row == source, 1.0, 0.0).astype(BF16)


def split_kernel(parts, tile_width, place_ref, tokens_ref, out_ref, onehot_ref):
    size = parts * tile_width
    rows = tokens_ref.shape[0]
    onehot_ref[...] = lane_regroup(parts, tile_width)
    me = place_ref[0]
    groups = tokens_ref.shape[1] // size
    lanes = jnp.concatenate(
        [tokens_ref[:, group * size : (group + 1) * size] for group in range(groups)], axis=0
    )
    picked = jnp.dot(lanes, onehot_ref[...], preferred_element_type=F32).astype(BF16)
    for part in range(parts):
        for group in range(groups):
            out_ref[me ^ part, :, group * tile_width : (group + 1) * tile_width] = picked[
                group * rows : (group + 1) * rows, part * tile_width : (part + 1) * tile_width
            ]


def join_kernel(parts, tile_width, groups_of, place_ref, onehot_ref, *refs):
    *part_refs, out_ref, held = refs
    size = parts * tile_width
    rows = out_ref.shape[0]
    me = place_ref[0]
    groups = out_ref.shape[1] // size
    first = 0
    for index, count in enumerate(groups_of):
        for step in range(count):
            own_ref, near_ref, far_ref = part_refs[3 * index : 3 * index + 3]
            total = own_ref[step] + near_ref[0, step].astype(F32) + far_ref[step].astype(F32)
            total = total.astype(BF16)
            for half in range(2):
                for group in range(groups):
                    at = (half * groups + group) * tile_width
                    held[me ^ (2 * (first + step) + half), group * rows : (group + 1) * rows] = (
                        total[:, at : at + tile_width]
                    )
        first += count
    lanes = jnp.concatenate([held[part] for part in range(parts)], axis=1)
    result = jnp.dot(lanes, onehot_ref[...], preferred_element_type=F32).astype(BF16)
    for group in range(groups):
        out_ref[:, group * size : (group + 1) * size] = result[group * rows : (group + 1) * rows]


def place_tiles(half, row_ref, col_ref, tiles_ref, out_ref, first=0):
    slots, rows, width = tiles_ref.shape
    start = half * (out_ref.shape[0] // 2)

    def place(slot, carry):
        top = pl.multiple_of(row_ref[0, first + slot] * rows + start, rows)
        left = pl.multiple_of(col_ref[0, first + slot] * width, width)
        out_ref[pl.ds(top, rows), pl.ds(left, width)] = tiles_ref[slot]
        return carry

    lax.fori_loop(0, slots, place, 0, unroll=15)


def weight_kernel(order_ref, row_ref, col_ref, own_ref, other_ref, w_ref):
    w_ref[...] = jnp.zeros_like(w_ref)
    place_tiles(0, row_ref, col_ref, own_ref, w_ref)
    place_tiles(1, row_ref, col_ref, other_ref, w_ref)


def early_kernel(n_tp, step, w_ref, *refs):
    x_refs = refs[:n_tp]
    *early_refs, sum_ref = refs[n_tp:]
    product = jnp.dot(slice_rows(x_refs, step), w_ref[...], preferred_element_type=F32)
    sum_ref[...] = product + early_refs[0][...] if early_refs else product


def halves_kernel(first_ref, second_ref, lower_ref, upper_ref):
    lower_ref[...] = first_ref[: lower_ref.shape[0]]
    upper_ref[...] = second_ref[lower_ref.shape[0] :]


def half_weight_kernel(order_ref, row_ref, col_ref, lower_ref, upper_ref, out_ref):
    out_ref[...] = jnp.zeros_like(out_ref)
    place_tiles(0, row_ref, col_ref, lower_ref, out_ref)
    place_tiles(0, row_ref, col_ref, upper_ref, out_ref, lower_ref.shape[0])


def gather_kernel(chips, n_tp, *refs):
    x_refs = refs[:n_tp]
    out_refs = refs[n_tp:]
    for step in range(chips):
        out_refs[step][...] = slice_rows(x_refs, step)


def transpose_kernel(order_ref, *refs):
    *part_refs, out_ref = refs
    out_ref[...] = jnp.concatenate([part_ref[...] for part_ref in part_refs], axis=0).T


def slice_rows(x_refs, step):
    return jnp.concatenate(
        [jnp.concatenate([x_ref[2 * step], x_ref[2 * step + 1]], axis=1) for x_ref in x_refs],
        axis=0,
    )


def hidden_kernel(n_tp, step, order_ref, z_ref, row_ref, col_ref, lower_ref, upper_ref, early_ref, cotangent_ref, half_ref, *refs):
    x_refs = refs[:n_tp]
    w_ref, act_ref, grad_ref = refs[n_tp:]
    rows = x_refs[0].shape[1]
    place_tiles(1, row_ref, col_ref, lower_ref, w_ref)
    place_tiles(1, row_ref, col_ref, upper_ref, w_ref, lower_ref.shape[0])
    lhs = slice_rows(x_refs, step)
    for left, right in column_blocks(w_ref.shape[1]):
        hidden = early_ref[:, left:right] + jnp.dot(
            lhs, w_ref[:, left:right], preferred_element_type=F32
        )
        act_value, act_slope = gelu_pair(hidden)
        act_value = act_value.astype(BF16)
        for j in range(n_tp):
            at = pl.ds(pl.multiple_of((z_ref[0] ^ j) * rows, rows), rows)
            act_ref[at, left:right] = act_value[j * rows : (j + 1) * rows]
            slope = act_slope[j * rows : (j + 1) * rows]
            grad_ref[j * rows : (j + 1) * rows, left:right] = (
                cotangent_ref[at, left:right].astype(F32) * slope
            ).astype(BF16)


def column_blocks(columns, block=512):
    return [(left, min(left + block, columns)) for left in range(0, columns, block)]


def back_kernel(n_tp, first, count, g_ref, *refs):
    w_refs = refs[:count]
    own_ref, near_ref, far_ref = refs[-3:]
    rows = g_ref.shape[0] // n_tp
    for step in range(count):
        result = lax.dot_general(
            g_ref[...], w_refs[step][...], (((1,), (1,)), ((), ())), preferred_element_type=F32
        )
        own_ref[first + step] = result[:rows]
        near_ref[0, first + step] = result[rows : 2 * rows].astype(BF16)
        near_ref[1, first + step] = result[3 * rows :].astype(BF16)
        far_ref[first + step] = result[2 * rows : 3 * rows]


def tile_grad_kernel(chips, scale, core_ref, row_ref, col_ref, x_ref, *refs):
    g_refs = refs[:chips]
    mine_ref, theirs_ref, dense = refs[chips:]
    slots, tile_rows, width = mine_ref.shape
    half = dense.shape[0] // 2
    for left, right in column_blocks(dense.shape[1]):
        g_all = jnp.concatenate([g_ref[:, left:right] for g_ref in g_refs], axis=0)
        dense[:, left:right] = jnp.dot(x_ref[...], g_all, preferred_element_type=F32)

    def place_tile(slot, carry):
        top = pl.multiple_of(row_ref[0, slot] * tile_rows, tile_rows)
        left = pl.multiple_of(col_ref[0, slot] * width, width)
        low = pl.multiple_of(top + half, tile_rows)
        mine_ref[slot] = dense[pl.ds(top, tile_rows), pl.ds(left, width)] * scale
        theirs_ref[slot] = (dense[pl.ds(low, tile_rows), pl.ds(left, width)] * scale).astype(
            theirs_ref.dtype
        )
        return carry

    lax.fori_loop(0, slots, place_tile, 0, unroll=15)


def params(limit):
    return pltpu.CompilerParams(vmem_limit_bytes=limit * MIB)


def cost(flops, bytes_accessed):
    return pl.CostEstimate(flops=flops >> 12, bytes_accessed=bytes_accessed >> 12, transcendentals=0)


def local(tokens, tile_values, tile_row, tile_col, grad_act):
    fsdp = lax.axis_size("fsdp")
    n_tp = lax.axis_size("tp")
    chips = fsdp // 2
    rows, width = tokens.shape
    tile_rows, slots, tile_width = tile_values.shape
    row_tiles = width // tile_width
    columns = grad_act.shape[1]
    col_tiles = columns // tile_width
    depth = row_tiles * 2 * tile_rows
    total_tokens = rows * fsdp * n_tp
    grad_scale = 1.0 / math.sqrt(total_tokens)
    place = lax.axis_index("fsdp")
    chip = place // 2
    core = place % 2
    z = lax.axis_index("tp")
    paired = n_tp & (n_tp - 1) == 0
    fast = (
        tile_rows % 16 == 0 and rows % 16 == 0 and row_tiles % fsdp == 0 and n_tp == 4 and chips == 4
    )

    def to_core(value):
        return lax.ppermute(value, "fsdp", [(f, f ^ 1) for f in range(fsdp)])

    def to_chip(value, step):
        return lax.ppermute(value, "fsdp", [(f, f ^ (2 * step)) for f in range(fsdp)])

    def to_z(value, step):
        if paired:
            return lax.ppermute(value, "tp", [(i, i ^ step) for i in range(n_tp)])
        return lax.ppermute(value, "tp", [(i, (i + step) % n_tp) for i in range(n_tp)])

    def from_z(value, step):
        return to_z(value, step if paired else n_tp - step)

    def z_rows(step):
        return (z ^ step if paired else (z - step) % n_tp) * rows

    def after(value, *earlier):
        return lax.optimization_barrier((value, *earlier))[0]

    def along_z(value):
        parts = [value]
        for j in range(1, n_tp):
            parts.append(to_z(parts[2], 1) if paired and j == 3 else to_z(value, j))
        return parts

    z_index = z.astype(jnp.int32).reshape(1)

    place_index = place.astype(jnp.int32).reshape(1)
    tiles = [jnp.transpose(tile_values, (1, 0, 2))]
    block = rows * n_tp
    if fast:
        def make_weight(step, order):
            return pl.pallas_call(
                weight_kernel,
                out_shape=jax.ShapeDtypeStruct((depth, columns), BF16),
                in_specs=[spec(SMEM)] * 3 + [spec()] * 2,
                out_specs=spec(),
                compiler_params=params(10),
                cost_estimate=cost(0, 2 * 2 * depth * columns),
            )(order, tile_row, tile_col, tiles[step], others[step])

        def add_hidden(step, *early):
            return pl.pallas_call(
                functools.partial(early_kernel, n_tp, step),
                out_shape=jax.ShapeDtypeStruct((block, columns), F32),
                in_specs=[spec()] * (1 + n_tp + len(early)),
                out_specs=spec(),
                compiler_params=params(14),
                cost_estimate=cost(2 * block * depth * columns, 2 * depth * columns),
            )(weights[step], *token_parts, *early)

        others = [to_core(tiles[0])]
        split, onehot = pl.pallas_call(
            functools.partial(split_kernel, fsdp, tile_width),
            out_shape=[
                jax.ShapeDtypeStruct((fsdp, rows, depth // 2), BF16),
                jax.ShapeDtypeStruct((fsdp * tile_width, fsdp * tile_width), BF16),
            ],
            in_specs=[spec(SMEM), spec()],
            out_specs=[spec()] * 2,
            compiler_params=params(8),
        )(place_index, tokens)
        token_parts = along_z(split)
        tiles += [to_chip(tiles[0], 1), to_chip(tiles[0], 2)]
        weights = [make_weight(0, z_index)]
        tiles[1], tiles[2], *_ = lax.optimization_barrier(
            (tiles[1], tiles[2], *token_parts[1:], weights[0])
        )
        half = slots // 2
        relay = pl.pallas_call(
            halves_kernel,
            out_shape=[
                jax.ShapeDtypeStruct((half, tile_rows, tile_width), BF16),
                jax.ShapeDtypeStruct((slots - half, tile_rows, tile_width), BF16),
            ],
            in_specs=[spec()] * 2,
            out_specs=[spec()] * 2,
            compiler_params=params(8),
        )(tiles[1], tiles[2])
        relayed = [to_chip(relay[0], 2), to_chip(relay[1], 1)]
        others += [to_core(part) for part in tiles[1:]]
        for step in range(1, chips - 1):
            weights.append(make_weight(step, after(z_index, weights[-1], *relay)))
        mine = pl.pallas_call(
            functools.partial(gather_kernel, chips, n_tp),
            out_shape=[jax.ShapeDtypeStruct((block, depth), BF16)] * chips,
            in_specs=[spec()] * n_tp,
            out_specs=[spec()] * chips,
            compiler_params=params(8),
        )(after(token_parts[0], weights[1]), *token_parts[1:])
        early = add_hidden(0)
        for step in range(1, chips - 1):
            early = add_hidden(step, early)
        *relayed, _ = lax.optimization_barrier((*relayed, early))
        last_others = [to_core(part) for part in relayed]
    else:
        tiles += [to_chip(tiles[0], step) for step in range(1, chips)]
        others = [to_core(part) for part in tiles]
        split = jnp.transpose(
            tokens.reshape(rows, row_tiles, chips, tile_width // chips), (2, 0, 1, 3)
        ).reshape(chips, rows, depth)
        split = jnp.take(split, jnp.arange(chips) ^ chip, axis=0)
        token_parts = along_z(split)
        pieces = [split[0]] + [to_chip(split[step], step) for step in range(1, chips)]
        slice_parts = along_z(jnp.stack(pieces))

    if fast:
        half_weight = pl.pallas_call(
            half_weight_kernel,
            out_shape=jax.ShapeDtypeStruct((depth, columns), BF16),
            in_specs=[spec(SMEM)] * 3 + [spec()] * 2,
            out_specs=spec(),
            compiler_params=params(10),
            cost_estimate=cost(0, 2 * 2 * depth * columns),
        )(z_index, tile_row, tile_col, *relayed)
        slices = pl.pallas_call(
            transpose_kernel,
            out_shape=jax.ShapeDtypeStruct((depth, chips * block), BF16),
            in_specs=[spec(SMEM)] + [spec()] * chips,
            out_specs=spec(),
            compiler_params=params(8),
        )(
            z_index,
            mine[0],
            *[to_chip(mine[step], step) for step in range(1, chips)],
        )
        last_weight, act, hidden_grad = pl.pallas_call(
            functools.partial(hidden_kernel, n_tp, chips - 1),
            out_shape=[
                jax.ShapeDtypeStruct((depth, columns), BF16),
                jax.ShapeDtypeStruct((block, columns), BF16),
                jax.ShapeDtypeStruct((block, columns), BF16),
            ],
            in_specs=[spec(SMEM)] * 4 + [spec()] * (5 + n_tp),
            out_specs=[spec()] * 3,
            input_output_aliases={8: 0},
            compiler_params=params(20),
            cost_estimate=cost(2 * block * depth * columns, 2 * depth * columns),
        )(
            after(z_index, slices), z_index, tile_row, tile_col, *last_others, early, grad_act, half_weight,
            *token_parts,
        )
        weights.append(last_weight)
    else:
        mine = jnp.stack(tiles, axis=1)
        theirs = jnp.stack(others, axis=1)
        both = jnp.where(
            core == 0,
            jnp.concatenate([mine, theirs], axis=2),
            jnp.concatenate([theirs, mine], axis=2),
        )
        flat = tile_row[0] * col_tiles + tile_col[0]
        weight = jnp.zeros((row_tiles * col_tiles, chips, 2 * tile_rows, tile_width), BF16)
        weight = weight.at[flat].set(both, unique_indices=True)
        weight = jnp.transpose(
            weight.reshape(row_tiles, col_tiles, chips, 2 * tile_rows, tile_width),
            (2, 0, 3, 1, 4),
        ).reshape(chips, depth, columns)
        hidden = jnp.einsum(
            "jqrk,qkc->jrc", jnp.stack(token_parts), weight, preferred_element_type=F32
        )
        act_value, act_slope = gelu_pair(hidden)
        act_value = act_value.astype(BF16)
        cotangent = jnp.stack(
            [lax.dynamic_slice_in_dim(grad_act, z_rows(j), rows, axis=0) for j in range(n_tp)]
        )
        hidden_grad = (cotangent.astype(F32) * act_slope).astype(BF16).reshape(block, columns)
        act = jnp.zeros((block, columns), BF16)
        for j in range(n_tp):
            act = lax.dynamic_update_slice_in_dim(act, act_value[j], z_rows(j), axis=0)

    grads = [hidden_grad] + [to_chip(hidden_grad, step) for step in range(1, chips)]

    if fast:
        group_sizes = (chips,)
        backs = []
        for first in range(0, chips, 2):
            backs = pl.pallas_call(
                functools.partial(back_kernel, n_tp, first, 2),
                out_shape=[
                    jax.ShapeDtypeStruct((chips, rows, depth), F32),
                    jax.ShapeDtypeStruct((2, chips, rows, depth), BF16),
                    jax.ShapeDtypeStruct((chips, rows, depth), F32),
                ],
                in_specs=[spec()] * (3 + len(backs)),
                out_specs=[spec()] * 3,
                input_output_aliases={3: 0, 4: 1, 5: 2} if backs else {},
                compiler_params=params(18),
                cost_estimate=cost(4 * block * depth * columns, 4 * depth * columns),
            )(hidden_grad, *weights[first : first + 2], *backs)
        near = to_z(backs[1], 1)
        far = to_z((backs[2] + near[1].astype(F32)).astype(BF16), 2)
        returned = [[backs[0], near, far]]
        grad_tokens = pl.pallas_call(
            functools.partial(join_kernel, fsdp, tile_width, group_sizes),
            out_shape=jax.ShapeDtypeStruct((rows, width), BF16),
            in_specs=[spec(SMEM)] + [spec()] * (1 + 3 * len(group_sizes)),
            out_specs=spec(),
            scratch_shapes=[pltpu.VMEM((fsdp, rows * row_tiles // fsdp, tile_width), BF16)],
            compiler_params=params(8),
        )(place_index, onehot, *[part for group in returned for part in group])
        mine, theirs = pl.pallas_call(
            functools.partial(tile_grad_kernel, chips, grad_scale),
            out_shape=[
                jax.ShapeDtypeStruct((slots, tile_rows, tile_width), F32),
                jax.ShapeDtypeStruct((slots, tile_rows, tile_width), BF16),
            ],
            in_specs=[spec(SMEM)] * 3 + [spec()] * (1 + chips),
            out_specs=[spec()] * 2,
            scratch_shapes=[pltpu.VMEM((depth, columns), F32)],
            compiler_params=params(26),
            cost_estimate=cost(2 * chips * block * depth * columns, 4 * depth * columns),
        )(z_index, tile_row, tile_col, slices, *grads)
        grad_tiles = mine + to_core(theirs).astype(F32)
    else:
        backs = jnp.einsum(
            "jrc,qkc->jqrk",
            hidden_grad.reshape(n_tp, rows, columns),
            weight,
            preferred_element_type=F32,
        )
        total = backs[0]
        for j in range(1, n_tp):
            total = total + from_z(backs[j].astype(BF16), j).astype(F32)
        joined = jnp.take(total.astype(BF16), jnp.arange(chips) ^ chip, axis=0)
        grad_tokens = jnp.transpose(
            joined.reshape(chips, rows, row_tiles, tile_width // chips), (1, 2, 0, 3)
        ).reshape(rows, width)
        x_all = jnp.stack(slice_parts, axis=1).reshape(-1, depth)
        g_all = jnp.stack(grads).reshape(-1, columns)
        dense = jnp.einsum("tk,tn->kn", x_all, g_all, preferred_element_type=F32) * grad_scale
        dense = jnp.transpose(
            dense.reshape(row_tiles, 2, tile_rows, col_tiles, tile_width), (1, 0, 3, 2, 4)
        ).reshape(2, row_tiles * col_tiles, tile_rows, tile_width)
        picked = jnp.take(dense, tile_row[0] * col_tiles + tile_col[0], axis=1)
        mine = jnp.where(core == 0, picked[0], picked[1])
        theirs = jnp.where(core == 0, picked[1], picked[0])
        grad_tiles = mine + to_core(theirs)
    grad_tiles = jnp.transpose(grad_tiles, (1, 0, 2))
    return (act, grad_tokens, grad_tiles)


def solution(mesh):
    in_specs = (
        P(("fsdp", "tp"), None),
        P("fsdp", "tp", None),
        P("tp", None),
        P("tp", None),
        P("fsdp", "tp"),
    )
    out_specs = (P("fsdp", "tp"), P(("fsdp", "tp"), None), P("fsdp", "tp", None))
    return jax.shard_map(local, mesh=mesh, in_specs=in_specs, out_specs=out_specs, check_vma=False)
```

```python
import functools
import math

import jax
import jax.numpy as jnp
from jax import lax
from jax.experimental import pallas as pl
from jax.experimental.pallas import tpu as pltpu
from jax.sharding import PartitionSpec as P

SQRT_TWO_PI = 0.7978845608028654
CUBIC_COEF = 0.044715
BF16 = jnp.bfloat16
F32 = jnp.float32
VMEM = pltpu.VMEM
SMEM = pltpu.SMEM
MIB = 1 << 20


def gelu_pair(pre_act):
    gelu_inner = SQRT_TWO_PI * (pre_act + CUBIC_COEF * pre_act * pre_act * pre_act)
    tanh_inner = jnp.tanh(gelu_inner)
    act_value = 0.5 * pre_act * (1.0 + tanh_inner)
    act_slope = 0.5 * (1.0 + tanh_inner) + 0.5 * pre_act * (
        1.0 - tanh_inner * tanh_inner
    ) * SQRT_TWO_PI * (1.0 + 3.0 * CUBIC_COEF * pre_act * pre_act)
    return (act_value, act_slope)


def spec(space=VMEM):
    return pl.BlockSpec(memory_space=space)


def lane_regroup(chips, tile_width):
    size = chips * tile_width
    part = tile_width // chips
    column = lax.broadcasted_iota(jnp.int32, (1, size), 1)
    chip = column // tile_width
    inner = column % tile_width
    source = (inner // part) * tile_width + chip * part + inner % part
    row = lax.broadcasted_iota(jnp.int32, (size, size), 0)
    return jnp.where(row == source, 1.0, 0.0).astype(BF16)


def split_kernel(parts, tile_width, place_ref, tokens_ref, out_ref, onehot_ref):
    size = parts * tile_width
    rows = tokens_ref.shape[0]
    onehot_ref[...] = lane_regroup(parts, tile_width)
    me = place_ref[0]
    groups = tokens_ref.shape[1] // size
    lanes = jnp.concatenate(
        [tokens_ref[:, group * size : (group + 1) * size] for group in range(groups)], axis=0
    )
    picked = jnp.dot(lanes, onehot_ref[...], preferred_element_type=F32).astype(BF16)
    for part in range(parts):
        for group in range(groups):
            out_ref[me ^ part, :, group * tile_width : (group + 1) * tile_width] = picked[
                group * rows : (group + 1) * rows, part * tile_width : (part + 1) * tile_width
            ]


def join_kernel(parts, tile_width, place_ref, onehot_ref, *refs):
    *part_refs, out_ref, held = refs
    size = parts * tile_width
    rows = out_ref.shape[0]
    me = place_ref[0]
    groups = out_ref.shape[1] // size
    for step in range(parts // 2):
        total = part_refs[0][step]
        for part_ref in part_refs[1:]:
            total = total + part_ref[step].astype(F32)
        total = total.astype(BF16)
        for half in range(2):
            for group in range(groups):
                at = (half * groups + group) * tile_width
                held[me ^ (2 * step + half), group * rows : (group + 1) * rows] = total[
                    :, at : at + tile_width
                ]
    lanes = jnp.concatenate([held[part] for part in range(parts)], axis=1)
    result = jnp.dot(lanes, onehot_ref[...], preferred_element_type=F32).astype(BF16)
    for group in range(groups):
        out_ref[:, group * size : (group + 1) * size] = result[group * rows : (group + 1) * rows]


def place_tiles(half, row_ref, col_ref, tiles_ref, out_ref, first=0, count=None):
    slots, rows, width = tiles_ref.shape
    slots = slots if count is None else count
    start = half * (out_ref.shape[0] // 2)

    def place(slot, carry):
        top = pl.multiple_of(row_ref[0, first + slot] * rows + start, rows)
        left = pl.multiple_of(col_ref[0, first + slot] * width, width)
        out_ref[pl.ds(top, rows), pl.ds(left, width)] = tiles_ref[slot]
        return carry

    lax.fori_loop(0, slots, place, 0, unroll=15)


def weight_kernel(order_ref, row_ref, col_ref, own_ref, other_ref, w_ref):
    w_ref[...] = jnp.zeros_like(w_ref)
    place_tiles(0, row_ref, col_ref, own_ref, w_ref)
    place_tiles(1, row_ref, col_ref, other_ref, w_ref)


def early_kernel(n_tp, step, w_ref, *refs):
    x_refs = refs[:n_tp]
    *early_refs, sum_ref = refs[n_tp:]
    product = jnp.dot(slice_rows(x_refs, step), w_ref[...], preferred_element_type=F32)
    sum_ref[...] = product + early_refs[0][...] if early_refs else product


def relay_kernel(first_ref, second_ref, lower_ref, upper_ref):
    lower_ref[...] = first_ref[: lower_ref.shape[0]]
    upper_ref[...] = second_ref[lower_ref.shape[0] :]


def half_weight_kernel(half, order_ref, row_ref, col_ref, lower_ref, upper_ref, out_ref):
    slots = row_ref.shape[1]
    out_ref[...] = jnp.zeros_like(out_ref)
    place_tiles(0, row_ref, col_ref, lower_ref, out_ref, 0, half)
    place_tiles(0, row_ref, col_ref, upper_ref, out_ref, half, slots - half)


def slice_rows(x_refs, step):
    return jnp.concatenate(
        [jnp.concatenate([x_ref[2 * step], x_ref[2 * step + 1]], axis=1) for x_ref in x_refs],
        axis=0,
    )


def hidden_kernel(n_tp, step, half, order_ref, z_ref, row_ref, col_ref, lower_ref, upper_ref, early_ref, cotangent_ref, half_ref, *refs):
    x_refs = refs[:n_tp]
    w_ref, act_ref, grad_ref, *pack_refs = refs[n_tp:]
    rows = x_refs[0].shape[1]
    place_tiles(1, row_ref, col_ref, lower_ref, w_ref, 0, half)
    place_tiles(1, row_ref, col_ref, upper_ref, w_ref, half, row_ref.shape[1] - half)
    lhs = slice_rows(x_refs, step)
    for left, right in column_blocks(w_ref.shape[1]):
        hidden = early_ref[:, left:right] + jnp.dot(
            lhs, w_ref[:, left:right], preferred_element_type=F32
        )
        act_value, act_slope = gelu_pair(hidden)
        act_value = act_value.astype(BF16)
        for j in range(n_tp):
            at = pl.ds(pl.multiple_of((z_ref[0] ^ j) * rows, rows), rows)
            act_ref[at, left:right] = act_value[j * rows : (j + 1) * rows]
            slope = act_slope[j * rows : (j + 1) * rows]
            grad = (cotangent_ref[at, left:right].astype(F32) * slope).astype(BF16)
            for out_ref in (grad_ref, *pack_refs):
                out_ref[j * rows : (j + 1) * rows, left:right] = grad
    for chip, pack_ref in enumerate(pack_refs):
        pack_ref[:, w_ref.shape[1] :] = slice_rows(x_refs, chip)


def column_blocks(columns, block=512):
    return [(left, min(left + block, columns)) for left in range(0, columns, block)]


def back_kernel(n_tp, first, count, g_ref, *refs):
    w_refs = refs[:count]
    out_refs = refs[-n_tp:]
    rows = g_ref.shape[0] // n_tp
    for step in range(count):
        result = lax.dot_general(
            w_refs[step][...], g_ref[...], (((1,), (1,)), ((), ())), preferred_element_type=F32
        ).T
        for j in range(n_tp):
            out_refs[j][first + step] = result[j * rows : (j + 1) * rows].astype(out_refs[j].dtype)


def tile_grad_kernel(chips, scale, order_ref, row_ref, col_ref, *refs):
    pack_refs = refs[:chips]
    mine_ref, theirs_ref, dense = refs[chips:]
    slots, tile_rows, width = mine_ref.shape
    columns = dense.shape[1]
    half = dense.shape[0] // 2
    x_t = jnp.concatenate([pack_ref[:, columns:] for pack_ref in pack_refs], axis=0).T
    for left, right in column_blocks(columns):
        g_all = jnp.concatenate([pack_ref[:, left:right] for pack_ref in pack_refs], axis=0)
        dense[:, left:right] = jnp.dot(x_t, g_all, preferred_element_type=F32)

    def place_tile(slot, carry):
        top = pl.multiple_of(row_ref[0, slot] * tile_rows, tile_rows)
        left = pl.multiple_of(col_ref[0, slot] * width, width)
        low = pl.multiple_of(top + half, tile_rows)
        mine_ref[slot] = dense[pl.ds(top, tile_rows), pl.ds(left, width)] * scale
        theirs_ref[slot] = (dense[pl.ds(low, tile_rows), pl.ds(left, width)] * scale).astype(
            theirs_ref.dtype
        )
        return carry

    lax.fori_loop(0, slots, place_tile, 0, unroll=15)


def params(limit):
    return pltpu.CompilerParams(vmem_limit_bytes=limit * MIB)


def cost(flops, bytes_accessed):
    return pl.CostEstimate(flops=flops >> 12, bytes_accessed=bytes_accessed >> 12, transcendentals=0)


def local(tokens, tile_values, tile_row, tile_col, grad_act):
    fsdp = lax.axis_size("fsdp")
    n_tp = lax.axis_size("tp")
    chips = fsdp // 2
    rows, width = tokens.shape
    tile_rows, slots, tile_width = tile_values.shape
    row_tiles = width // tile_width
    columns = grad_act.shape[1]
    col_tiles = columns // tile_width
    depth = row_tiles * 2 * tile_rows
    total_tokens = rows * fsdp * n_tp
    grad_scale = 1.0 / math.sqrt(total_tokens)
    place = lax.axis_index("fsdp")
    chip = place // 2
    core = place % 2
    z = lax.axis_index("tp")
    paired = n_tp & (n_tp - 1) == 0
    fast = (
        tile_rows % 16 == 0 and rows % 16 == 0 and row_tiles % fsdp == 0 and n_tp == 4 and chips == 4
    )

    def to_core(value):
        return lax.ppermute(value, "fsdp", [(f, f ^ 1) for f in range(fsdp)])

    def to_chip(value, step):
        return lax.ppermute(value, "fsdp", [(f, f ^ (2 * step)) for f in range(fsdp)])

    def to_z(value, step):
        if paired:
            return lax.ppermute(value, "tp", [(i, i ^ step) for i in range(n_tp)])
        return lax.ppermute(value, "tp", [(i, (i + step) % n_tp) for i in range(n_tp)])

    def from_z(value, step):
        return to_z(value, step if paired else n_tp - step)

    def z_rows(step):
        return (z ^ step if paired else (z - step) % n_tp) * rows

    def after(value, *earlier):
        return lax.optimization_barrier((value, *earlier))[0]

    def along_z(value):
        parts = [value]
        for j in range(1, n_tp):
            parts.append(to_z(parts[2], 1) if paired and j == 3 else to_z(value, j))
        return parts

    z_index = z.astype(jnp.int32).reshape(1)

    place_index = place.astype(jnp.int32).reshape(1)
    tiles = [jnp.transpose(tile_values, (1, 0, 2))]
    block = rows * n_tp
    if fast:
        def make_weight(step, order):
            return pl.pallas_call(
                weight_kernel,
                out_shape=jax.ShapeDtypeStruct((depth, columns), BF16),
                in_specs=[spec(SMEM)] * 3 + [spec()] * 2,
                out_specs=spec(),
                compiler_params=params(10),
                cost_estimate=cost(0, 2 * 2 * depth * columns),
            )(order, tile_row, tile_col, tiles[step], others[step])

        def add_hidden(step, *early):
            return pl.pallas_call(
                functools.partial(early_kernel, n_tp, step),
                out_shape=jax.ShapeDtypeStruct((block, columns), F32),
                in_specs=[spec()] * (1 + n_tp + len(early)),
                out_specs=spec(),
                compiler_params=params(14),
                cost_estimate=cost(2 * block * depth * columns, 2 * depth * columns),
            )(weights[step], *token_parts, *early)

        others = [to_core(tiles[0])]
        split, onehot = pl.pallas_call(
            functools.partial(split_kernel, fsdp, tile_width),
            out_shape=[
                jax.ShapeDtypeStruct((fsdp, rows, depth // 2), BF16),
                jax.ShapeDtypeStruct((fsdp * tile_width, fsdp * tile_width), BF16),
            ],
            in_specs=[spec(SMEM), spec()],
            out_specs=[spec()] * 2,
            compiler_params=params(8),
        )(place_index, tokens)
        token_parts = along_z(split)
        tiles += [to_chip(tiles[0], 1), to_chip(tiles[0], 2)]
        weights = [make_weight(0, z_index)]
        tiles[1], tiles[2], *_ = lax.optimization_barrier(
            (tiles[1], tiles[2], *token_parts[1:], weights[0])
        )
        half = slots // 2
        relay = pl.pallas_call(
            relay_kernel,
            out_shape=[
                jax.ShapeDtypeStruct((half, tile_rows, tile_width), BF16),
                jax.ShapeDtypeStruct((slots - half, tile_rows, tile_width), BF16),
            ],
            in_specs=[spec()] * 2,
            out_specs=[spec()] * 2,
            compiler_params=params(8),
        )(tiles[1], tiles[2])
        relayed = [to_chip(relay[0], 2), to_chip(relay[1], 1)]
        others += [to_core(part) for part in tiles[1:]]
        for step in range(1, chips - 1):
            weights.append(make_weight(step, after(z_index, weights[-1], *relay)))
        early = add_hidden(0)
        for step in range(1, chips - 1):
            early = add_hidden(step, early)
        *relayed, _ = lax.optimization_barrier((*relayed, early))
        last_others = [to_core(part) for part in relayed]
    else:
        tiles += [to_chip(tiles[0], step) for step in range(1, chips)]
        others = [to_core(part) for part in tiles]
        split = jnp.transpose(
            tokens.reshape(rows, row_tiles, chips, tile_width // chips), (2, 0, 1, 3)
        ).reshape(chips, rows, depth)
        split = jnp.take(split, jnp.arange(chips) ^ chip, axis=0)
        token_parts = along_z(split)
        pieces = [split[0]] + [to_chip(split[step], step) for step in range(1, chips)]
        slice_parts = along_z(jnp.stack(pieces))

    if fast:
        half_weight = pl.pallas_call(
            functools.partial(half_weight_kernel, half),
            out_shape=jax.ShapeDtypeStruct((depth, columns), BF16),
            in_specs=[spec(SMEM)] * 3 + [spec()] * 2,
            out_specs=spec(),
            compiler_params=params(10),
            cost_estimate=cost(0, 2 * 2 * depth * columns),
        )(z_index, tile_row, tile_col, *relayed)
        last_weight, act, hidden_grad, *packs = pl.pallas_call(
            functools.partial(hidden_kernel, n_tp, chips - 1, half),
            out_shape=[
                jax.ShapeDtypeStruct((depth, columns), BF16),
                jax.ShapeDtypeStruct((block, columns), BF16),
                jax.ShapeDtypeStruct((block, columns), BF16),
            ]
            + [jax.ShapeDtypeStruct((block, columns + depth), BF16)] * chips,
            in_specs=[spec(SMEM)] * 4 + [spec()] * (5 + n_tp),
            out_specs=[spec()] * (3 + chips),
            input_output_aliases={8: 0},
            compiler_params=params(24),
            cost_estimate=cost(2 * block * depth * columns, 2 * depth * columns),
        )(
            z_index, z_index, tile_row, tile_col, *last_others, early, grad_act, half_weight,
            *token_parts,
        )
        weights.append(last_weight)
    else:
        mine = jnp.stack(tiles, axis=1)
        theirs = jnp.stack(others, axis=1)
        both = jnp.where(
            core == 0,
            jnp.concatenate([mine, theirs], axis=2),
            jnp.concatenate([theirs, mine], axis=2),
        )
        flat = tile_row[0] * col_tiles + tile_col[0]
        weight = jnp.zeros((row_tiles * col_tiles, chips, 2 * tile_rows, tile_width), BF16)
        weight = weight.at[flat].set(both, unique_indices=True)
        weight = jnp.transpose(
            weight.reshape(row_tiles, col_tiles, chips, 2 * tile_rows, tile_width),
            (2, 0, 3, 1, 4),
        ).reshape(chips, depth, columns)
        hidden = jnp.einsum(
            "jqrk,qkc->jrc", jnp.stack(token_parts), weight, preferred_element_type=F32
        )
        act_value, act_slope = gelu_pair(hidden)
        act_value = act_value.astype(BF16)
        cotangent = jnp.stack(
            [lax.dynamic_slice_in_dim(grad_act, z_rows(j), rows, axis=0) for j in range(n_tp)]
        )
        hidden_grad = (cotangent.astype(F32) * act_slope).astype(BF16).reshape(block, columns)
        act = jnp.zeros((block, columns), BF16)
        for j in range(n_tp):
            act = lax.dynamic_update_slice_in_dim(act, act_value[j], z_rows(j), axis=0)


    if fast:
        packs = [packs[0]] + [to_chip(packs[step], step) for step in range(1, chips)]
        backs = []
        for first in range(0, chips, 2):
            backs = pl.pallas_call(
                functools.partial(back_kernel, n_tp, first, 2),
                out_shape=[
                    jax.ShapeDtypeStruct((chips, rows, depth), F32 if j == 0 else BF16)
                    for j in range(n_tp)
                ],
                in_specs=[spec()] * (3 + len(backs)),
                out_specs=[spec()] * n_tp,
                input_output_aliases={3 + j: j for j in range(n_tp)} if backs else {},
                compiler_params=params(18),
                cost_estimate=cost(4 * block * depth * columns, 4 * depth * columns),
            )(hidden_grad, *weights[first : first + 2], *backs)
        returned = [backs[0]] + [to_z(backs[j], j) for j in range(1, n_tp)]
        mine, theirs = pl.pallas_call(
            functools.partial(tile_grad_kernel, chips, grad_scale),
            out_shape=[
                jax.ShapeDtypeStruct((slots, tile_rows, tile_width), F32),
                jax.ShapeDtypeStruct((slots, tile_rows, tile_width), BF16),
            ],
            in_specs=[spec(SMEM)] * 3 + [spec()] * chips,
            out_specs=[spec()] * 2,
            scratch_shapes=[pltpu.VMEM((depth, columns), F32)],
            compiler_params=params(28),
            cost_estimate=cost(2 * chips * block * depth * columns, 4 * depth * columns),
        )(after(z_index, *returned[1:]), tile_row, tile_col, *packs)
        grad_tiles = mine + to_core(theirs).astype(F32)
        grad_tokens = pl.pallas_call(
            functools.partial(join_kernel, fsdp, tile_width),
            out_shape=jax.ShapeDtypeStruct((rows, width), BF16),
            in_specs=[spec(SMEM)] + [spec()] * (1 + n_tp),
            out_specs=spec(),
            scratch_shapes=[pltpu.VMEM((fsdp, rows * row_tiles // fsdp, tile_width), BF16)],
            compiler_params=params(8),
        )(place_index, onehot, *returned)
    else:
        grads = [hidden_grad] + [to_chip(hidden_grad, step) for step in range(1, chips)]
        backs = jnp.einsum(
            "jrc,qkc->jqrk",
            hidden_grad.reshape(n_tp, rows, columns),
            weight,
            preferred_element_type=F32,
        )
        total = backs[0]
        for j in range(1, n_tp):
            total = total + from_z(backs[j].astype(BF16), j).astype(F32)
        joined = jnp.take(total.astype(BF16), jnp.arange(chips) ^ chip, axis=0)
        grad_tokens = jnp.transpose(
            joined.reshape(chips, rows, row_tiles, tile_width // chips), (1, 2, 0, 3)
        ).reshape(rows, width)
        x_all = jnp.stack(slice_parts, axis=1).reshape(-1, depth)
        g_all = jnp.stack(grads).reshape(-1, columns)
        dense = jnp.einsum("tk,tn->kn", x_all, g_all, preferred_element_type=F32) * grad_scale
        dense = jnp.transpose(
            dense.reshape(row_tiles, 2, tile_rows, col_tiles, tile_width), (1, 0, 3, 2, 4)
        ).reshape(2, row_tiles * col_tiles, tile_rows, tile_width)
        picked = jnp.take(dense, tile_row[0] * col_tiles + tile_col[0], axis=1)
        mine = jnp.where(core == 0, picked[0], picked[1])
        theirs = jnp.where(core == 0, picked[1], picked[0])
        grad_tiles = mine + to_core(theirs)
    grad_tiles = jnp.transpose(grad_tiles, (1, 0, 2))
    return (act, grad_tokens, grad_tiles)


def solution(mesh):
    in_specs = (
        P(("fsdp", "tp"), None),
        P("fsdp", "tp", None),
        P("tp", None),
        P("tp", None),
        P("fsdp", "tp"),
    )
    out_specs = (P("fsdp", "tp"), P(("fsdp", "tp"), None), P("fsdp", "tp", None))
    return jax.shard_map(local, mesh=mesh, in_specs=in_specs, out_specs=out_specs, check_vma=False)
```

```python
import functools
import math

import jax
import jax.numpy as jnp
from jax import lax
from jax.experimental import pallas as pl
from jax.experimental.pallas import tpu as pltpu
from jax.sharding import PartitionSpec as P

SQRT_TWO_PI = 0.7978845608028654
CUBIC_COEF = 0.044715
BF16 = jnp.bfloat16
F32 = jnp.float32
VMEM = pltpu.VMEM
SMEM = pltpu.SMEM
MIB = 1 << 20


def gelu_pair(pre_act):
    gelu_inner = SQRT_TWO_PI * (pre_act + CUBIC_COEF * pre_act * pre_act * pre_act)
    tanh_inner = jnp.tanh(gelu_inner)
    act_value = 0.5 * pre_act * (1.0 + tanh_inner)
    act_slope = 0.5 * (1.0 + tanh_inner) + 0.5 * pre_act * (
        1.0 - tanh_inner * tanh_inner
    ) * SQRT_TWO_PI * (1.0 + 3.0 * CUBIC_COEF * pre_act * pre_act)
    return (act_value, act_slope)


def spec(space=VMEM):
    return pl.BlockSpec(memory_space=space)


def lane_regroup(chips, tile_width):
    size = chips * tile_width
    part = tile_width // chips
    column = lax.broadcasted_iota(jnp.int32, (1, size), 1)
    chip = column // tile_width
    inner = column % tile_width
    source = (inner // part) * tile_width + chip * part + inner % part
    row = lax.broadcasted_iota(jnp.int32, (size, size), 0)
    return jnp.where(row == source, 1.0, 0.0).astype(BF16)


def split_kernel(parts, tile_width, place_ref, tokens_ref, out_ref, onehot_ref):
    size = parts * tile_width
    rows = tokens_ref.shape[0]
    onehot_ref[...] = lane_regroup(parts, tile_width)
    me = place_ref[0]
    groups = tokens_ref.shape[1] // size
    lanes = jnp.concatenate(
        [tokens_ref[:, group * size : (group + 1) * size] for group in range(groups)], axis=0
    )
    picked = jnp.dot(lanes, onehot_ref[...], preferred_element_type=F32).astype(BF16)
    for part in range(parts):
        for group in range(groups):
            out_ref[me ^ part, :, group * tile_width : (group + 1) * tile_width] = picked[
                group * rows : (group + 1) * rows, part * tile_width : (part + 1) * tile_width
            ]


def join_kernel(parts, tile_width, place_ref, onehot_ref, *refs):
    *part_refs, out_ref, held = refs
    size = parts * tile_width
    rows = out_ref.shape[0]
    me = place_ref[0]
    groups = out_ref.shape[1] // size
    for step in range(parts // 2):
        total = part_refs[0][step]
        for part_ref in part_refs[1:]:
            total = total + part_ref[step].astype(F32)
        total = total.astype(BF16)
        for half in range(2):
            for group in range(groups):
                at = (half * groups + group) * tile_width
                held[me ^ (2 * step + half), group * rows : (group + 1) * rows] = total[
                    :, at : at + tile_width
                ]
    lanes = jnp.concatenate([held[part] for part in range(parts)], axis=1)
    result = jnp.dot(lanes, onehot_ref[...], preferred_element_type=F32).astype(BF16)
    for group in range(groups):
        out_ref[:, group * size : (group + 1) * size] = result[group * rows : (group + 1) * rows]


def place_tiles(half, row_ref, col_ref, tiles_ref, out_ref, first=0, count=None):
    slots, rows, width = tiles_ref.shape
    slots = slots if count is None else count
    start = half * (out_ref.shape[0] // 2)

    def place(slot, carry):
        top = pl.multiple_of(row_ref[0, first + slot] * rows + start, rows)
        left = pl.multiple_of(col_ref[0, first + slot] * width, width)
        out_ref[pl.ds(top, rows), pl.ds(left, width)] = tiles_ref[slot]
        return carry

    lax.fori_loop(0, slots, place, 0, unroll=15)


def weight_kernel(order_ref, row_ref, col_ref, own_ref, other_ref, w_ref):
    w_ref[...] = jnp.zeros_like(w_ref)
    place_tiles(0, row_ref, col_ref, own_ref, w_ref)
    place_tiles(1, row_ref, col_ref, other_ref, w_ref)


def early_kernel(n_tp, step, w_ref, *refs):
    x_refs = refs[:n_tp]
    *early_refs, sum_ref = refs[n_tp:]
    product = jnp.dot(slice_rows(x_refs, step), w_ref[...], preferred_element_type=F32)
    sum_ref[...] = product + early_refs[0][...] if early_refs else product


def relay_kernel(first_ref, second_ref, lower_ref, upper_ref):
    lower_ref[...] = first_ref[: lower_ref.shape[0]]
    upper_ref[...] = second_ref[lower_ref.shape[0] :]


def blank_kernel(order_ref, out_ref):
    out_ref[...] = jnp.zeros_like(out_ref)


def half_weight_kernel(n_tp, step, half, order_ref, row_ref, col_ref, lower_ref, upper_ref, blank_ref, early_ref, *refs):
    x_refs = refs[:n_tp]
    out_ref, sum_ref = refs[n_tp:]
    slots = row_ref.shape[1]
    rows = out_ref.shape[0] // 2
    place_tiles(0, row_ref, col_ref, lower_ref, out_ref, 0, half)
    place_tiles(0, row_ref, col_ref, upper_ref, out_ref, half, slots - half)
    lhs = jnp.concatenate([x_ref[2 * step] for x_ref in x_refs], axis=0)
    sum_ref[...] = early_ref[...] + jnp.dot(
        lhs, out_ref[:rows, :], preferred_element_type=F32
    )


def slice_rows(x_refs, step):
    return jnp.concatenate(
        [jnp.concatenate([x_ref[2 * step], x_ref[2 * step + 1]], axis=1) for x_ref in x_refs],
        axis=0,
    )


def hidden_kernel(n_tp, step, half, order_ref, z_ref, row_ref, col_ref, lower_ref, upper_ref, early_ref, cotangent_ref, half_ref, *refs):
    x_refs = refs[:n_tp]
    w_ref, act_ref, grad_ref, *pack_refs = refs[n_tp:]
    rows = x_refs[0].shape[1]
    place_tiles(1, row_ref, col_ref, lower_ref, w_ref, 0, half)
    place_tiles(1, row_ref, col_ref, upper_ref, w_ref, half, row_ref.shape[1] - half)
    half_rows = w_ref.shape[0] // 2
    lhs = jnp.concatenate([x_ref[2 * step + 1] for x_ref in x_refs], axis=0)
    for left, right in column_blocks(w_ref.shape[1]):
        hidden = early_ref[:, left:right] + jnp.dot(
            lhs, w_ref[half_rows:, left:right], preferred_element_type=F32
        )
        act_value, act_slope = gelu_pair(hidden)
        act_value = act_value.astype(BF16)
        for j in range(n_tp):
            at = pl.ds(pl.multiple_of((z_ref[0] ^ j) * rows, rows), rows)
            act_ref[at, left:right] = act_value[j * rows : (j + 1) * rows]
            slope = act_slope[j * rows : (j + 1) * rows]
            grad = (cotangent_ref[at, left:right].astype(F32) * slope).astype(BF16)
            for out_ref in (grad_ref, *pack_refs):
                out_ref[j * rows : (j + 1) * rows, left:right] = grad
    for chip, pack_ref in enumerate(pack_refs):
        pack_ref[:, w_ref.shape[1] :] = slice_rows(x_refs, chip)


def column_blocks(columns, block=512):
    return [(left, min(left + block, columns)) for left in range(0, columns, block)]


def back_kernel(n_tp, first, count, g_ref, *refs):
    w_refs = refs[:count]
    out_refs = refs[-n_tp:]
    rows = g_ref.shape[0] // n_tp
    for step in range(count):
        result = lax.dot_general(
            w_refs[step][...], g_ref[...], (((1,), (1,)), ((), ())), preferred_element_type=F32
        ).T
        for j in range(n_tp):
            out_refs[j][first + step] = result[j * rows : (j + 1) * rows].astype(out_refs[j].dtype)


def tile_grad_kernel(chips, scale, order_ref, row_ref, col_ref, *refs):
    pack_refs = refs[:chips]
    mine_ref, theirs_ref, dense = refs[chips:]
    slots, tile_rows, width = mine_ref.shape
    columns = dense.shape[1]
    half = dense.shape[0] // 2
    x_t = jnp.concatenate([pack_ref[:, columns:] for pack_ref in pack_refs], axis=0).T
    for left, right in column_blocks(columns):
        g_all = jnp.concatenate([pack_ref[:, left:right] for pack_ref in pack_refs], axis=0)
        dense[:, left:right] = jnp.dot(x_t, g_all, preferred_element_type=F32)

    def place_tile(slot, carry):
        top = pl.multiple_of(row_ref[0, slot] * tile_rows, tile_rows)
        left = pl.multiple_of(col_ref[0, slot] * width, width)
        low = pl.multiple_of(top + half, tile_rows)
        mine_ref[slot] = dense[pl.ds(top, tile_rows), pl.ds(left, width)] * scale
        theirs_ref[slot] = (dense[pl.ds(low, tile_rows), pl.ds(left, width)] * scale).astype(
            theirs_ref.dtype
        )
        return carry

    lax.fori_loop(0, slots, place_tile, 0, unroll=15)


def params(limit):
    return pltpu.CompilerParams(vmem_limit_bytes=limit * MIB)


def cost(flops, bytes_accessed):
    return pl.CostEstimate(flops=flops >> 12, bytes_accessed=bytes_accessed >> 12, transcendentals=0)


def local(tokens, tile_values, tile_row, tile_col, grad_act):
    fsdp = lax.axis_size("fsdp")
    n_tp = lax.axis_size("tp")
    chips = fsdp // 2
    rows, width = tokens.shape
    tile_rows, slots, tile_width = tile_values.shape
    row_tiles = width // tile_width
    columns = grad_act.shape[1]
    col_tiles = columns // tile_width
    depth = row_tiles * 2 * tile_rows
    total_tokens = rows * fsdp * n_tp
    grad_scale = 1.0 / math.sqrt(total_tokens)
    place = lax.axis_index("fsdp")
    chip = place // 2
    core = place % 2
    z = lax.axis_index("tp")
    paired = n_tp & (n_tp - 1) == 0
    fast = (
        tile_rows % 16 == 0 and rows % 16 == 0 and row_tiles % fsdp == 0 and n_tp == 4 and chips == 4
    )

    def to_core(value):
        return lax.ppermute(value, "fsdp", [(f, f ^ 1) for f in range(fsdp)])

    def to_chip(value, step):
        return lax.ppermute(value, "fsdp", [(f, f ^ (2 * step)) for f in range(fsdp)])

    def to_z(value, step):
        if paired:
            return lax.ppermute(value, "tp", [(i, i ^ step) for i in range(n_tp)])
        return lax.ppermute(value, "tp", [(i, (i + step) % n_tp) for i in range(n_tp)])

    def from_z(value, step):
        return to_z(value, step if paired else n_tp - step)

    def z_rows(step):
        return (z ^ step if paired else (z - step) % n_tp) * rows

    def after(value, *earlier):
        return lax.optimization_barrier((value, *earlier))[0]

    def along_z(value):
        parts = [value]
        for j in range(1, n_tp):
            parts.append(to_z(parts[2], 1) if paired and j == 3 else to_z(value, j))
        return parts

    z_index = z.astype(jnp.int32).reshape(1)

    place_index = place.astype(jnp.int32).reshape(1)
    tiles = [jnp.transpose(tile_values, (1, 0, 2))]
    block = rows * n_tp
    if fast:
        def make_weight(step, order):
            return pl.pallas_call(
                weight_kernel,
                out_shape=jax.ShapeDtypeStruct((depth, columns), BF16),
                in_specs=[spec(SMEM)] * 3 + [spec()] * 2,
                out_specs=spec(),
                compiler_params=params(10),
                cost_estimate=cost(0, 2 * 2 * depth * columns),
            )(order, tile_row, tile_col, tiles[step], others[step])

        def add_hidden(step, *early):
            return pl.pallas_call(
                functools.partial(early_kernel, n_tp, step),
                out_shape=jax.ShapeDtypeStruct((block, columns), F32),
                in_specs=[spec()] * (1 + n_tp + len(early)),
                out_specs=spec(),
                compiler_params=params(14),
                cost_estimate=cost(2 * block * depth * columns, 2 * depth * columns),
            )(weights[step], *token_parts, *early)

        others = [to_core(tiles[0])]
        split, onehot = pl.pallas_call(
            functools.partial(split_kernel, fsdp, tile_width),
            out_shape=[
                jax.ShapeDtypeStruct((fsdp, rows, depth // 2), BF16),
                jax.ShapeDtypeStruct((fsdp * tile_width, fsdp * tile_width), BF16),
            ],
            in_specs=[spec(SMEM), spec()],
            out_specs=[spec()] * 2,
            compiler_params=params(8),
        )(place_index, tokens)
        token_parts = along_z(split)
        tiles += [to_chip(tiles[0], 1), to_chip(tiles[0], 2)]
        weights = [make_weight(0, z_index)]
        blank = pl.pallas_call(
            blank_kernel,
            out_shape=jax.ShapeDtypeStruct((depth, columns), BF16),
            in_specs=[spec(SMEM)],
            out_specs=spec(),
            compiler_params=params(10),
            cost_estimate=cost(0, 2 * depth * columns),
        )(after(z_index, weights[0]))
        tiles[1], tiles[2], blank, *_ = lax.optimization_barrier(
            (tiles[1], tiles[2], blank, *token_parts[1:], weights[0])
        )
        half = slots // 2
        relay = pl.pallas_call(
            relay_kernel,
            out_shape=[
                jax.ShapeDtypeStruct((half, tile_rows, tile_width), BF16),
                jax.ShapeDtypeStruct((slots - half, tile_rows, tile_width), BF16),
            ],
            in_specs=[spec()] * 2,
            out_specs=[spec()] * 2,
            compiler_params=params(8),
        )(tiles[1], tiles[2])
        relayed = [to_chip(relay[0], 2), to_chip(relay[1], 1)]
        others += [to_core(after(part, *relay)) for part in tiles[1:]]
        for step in range(1, chips - 1):
            weights.append(make_weight(step, after(z_index, weights[-1], *relay)))
        early = add_hidden(0)
        for step in range(1, chips - 1):
            early = add_hidden(step, early)
        *relayed, _ = lax.optimization_barrier((*relayed, early))
        last_others = [to_core(part) for part in relayed]
    else:
        tiles += [to_chip(tiles[0], step) for step in range(1, chips)]
        others = [to_core(part) for part in tiles]
        split = jnp.transpose(
            tokens.reshape(rows, row_tiles, chips, tile_width // chips), (2, 0, 1, 3)
        ).reshape(chips, rows, depth)
        split = jnp.take(split, jnp.arange(chips) ^ chip, axis=0)
        token_parts = along_z(split)
        pieces = [split[0]] + [to_chip(split[step], step) for step in range(1, chips)]
        slice_parts = along_z(jnp.stack(pieces))

    if fast:
        half_weight, early = pl.pallas_call(
            functools.partial(half_weight_kernel, n_tp, chips - 1, half),
            out_shape=[
                jax.ShapeDtypeStruct((depth, columns), BF16),
                jax.ShapeDtypeStruct((block, columns), F32),
            ],
            in_specs=[spec(SMEM)] * 3 + [spec()] * (4 + n_tp),
            out_specs=[spec()] * 2,
            input_output_aliases={5: 0, 6: 1},
            compiler_params=params(20),
            cost_estimate=cost(block * depth * columns, 2 * depth * columns),
        )(z_index, tile_row, tile_col, *relayed, blank, early, *token_parts)
        last_weight, act, hidden_grad, *packs = pl.pallas_call(
            functools.partial(hidden_kernel, n_tp, chips - 1, half),
            out_shape=[
                jax.ShapeDtypeStruct((depth, columns), BF16),
                jax.ShapeDtypeStruct((block, columns), BF16),
                jax.ShapeDtypeStruct((block, columns), BF16),
            ]
            + [jax.ShapeDtypeStruct((block, columns + depth), BF16)] * chips,
            in_specs=[spec(SMEM)] * 4 + [spec()] * (5 + n_tp),
            out_specs=[spec()] * (3 + chips),
            input_output_aliases={8: 0},
            compiler_params=params(24),
            cost_estimate=cost(2 * block * depth * columns, 2 * depth * columns),
        )(
            z_index, z_index, tile_row, tile_col, *last_others, early, grad_act, half_weight,
            *token_parts,
        )
        weights.append(last_weight)
    else:
        mine = jnp.stack(tiles, axis=1)
        theirs = jnp.stack(others, axis=1)
        both = jnp.where(
            core == 0,
            jnp.concatenate([mine, theirs], axis=2),
            jnp.concatenate([theirs, mine], axis=2),
        )
        flat = tile_row[0] * col_tiles + tile_col[0]
        weight = jnp.zeros((row_tiles * col_tiles, chips, 2 * tile_rows, tile_width), BF16)
        weight = weight.at[flat].set(both, unique_indices=True)
        weight = jnp.transpose(
            weight.reshape(row_tiles, col_tiles, chips, 2 * tile_rows, tile_width),
            (2, 0, 3, 1, 4),
        ).reshape(chips, depth, columns)
        hidden = jnp.einsum(
            "jqrk,qkc->jrc", jnp.stack(token_parts), weight, preferred_element_type=F32
        )
        act_value, act_slope = gelu_pair(hidden)
        act_value = act_value.astype(BF16)
        cotangent = jnp.stack(
            [lax.dynamic_slice_in_dim(grad_act, z_rows(j), rows, axis=0) for j in range(n_tp)]
        )
        hidden_grad = (cotangent.astype(F32) * act_slope).astype(BF16).reshape(block, columns)
        act = jnp.zeros((block, columns), BF16)
        for j in range(n_tp):
            act = lax.dynamic_update_slice_in_dim(act, act_value[j], z_rows(j), axis=0)


    if fast:
        packs = [packs[0]] + [to_chip(packs[step], step) for step in range(1, chips)]
        backs = []
        for first in range(0, chips, 2):
            backs = pl.pallas_call(
                functools.partial(back_kernel, n_tp, first, 2),
                out_shape=[
                    jax.ShapeDtypeStruct((chips, rows, depth), F32 if j == 0 else BF16)
                    for j in range(n_tp)
                ],
                in_specs=[spec()] * (3 + len(backs)),
                out_specs=[spec()] * n_tp,
                input_output_aliases={3 + j: j for j in range(n_tp)} if backs else {},
                compiler_params=params(18),
                cost_estimate=cost(4 * block * depth * columns, 4 * depth * columns),
            )(hidden_grad, *weights[first : first + 2], *backs)
        near = after(backs[1], packs[1])
        returned = [backs[0]] + [
            to_z(near if j == 1 else backs[j], j) for j in range(1, n_tp)
        ]
        mine, theirs = pl.pallas_call(
            functools.partial(tile_grad_kernel, chips, grad_scale),
            out_shape=[
                jax.ShapeDtypeStruct((slots, tile_rows, tile_width), F32),
                jax.ShapeDtypeStruct((slots, tile_rows, tile_width), BF16),
            ],
            in_specs=[spec(SMEM)] * 3 + [spec()] * chips,
            out_specs=[spec()] * 2,
            scratch_shapes=[pltpu.VMEM((depth, columns), F32)],
            compiler_params=params(28),
            cost_estimate=cost(2 * chips * block * depth * columns, 4 * depth * columns),
        )(after(z_index, *returned[1:]), tile_row, tile_col, *packs)
        grad_tiles = mine + to_core(theirs).astype(F32)
        grad_tokens = pl.pallas_call(
            functools.partial(join_kernel, fsdp, tile_width),
            out_shape=jax.ShapeDtypeStruct((rows, width), BF16),
            in_specs=[spec(SMEM)] + [spec()] * (1 + n_tp),
            out_specs=spec(),
            scratch_shapes=[pltpu.VMEM((fsdp, rows * row_tiles // fsdp, tile_width), BF16)],
            compiler_params=params(8),
        )(place_index, onehot, *returned)
    else:
        grads = [hidden_grad] + [to_chip(hidden_grad, step) for step in range(1, chips)]
        backs = jnp.einsum(
            "jrc,qkc->jqrk",
            hidden_grad.reshape(n_tp, rows, columns),
            weight,
            preferred_element_type=F32,
        )
        total = backs[0]
        for j in range(1, n_tp):
            total = total + from_z(backs[j].astype(BF16), j).astype(F32)
        joined = jnp.take(total.astype(BF16), jnp.arange(chips) ^ chip, axis=0)
        grad_tokens = jnp.transpose(
            joined.reshape(chips, rows, row_tiles, tile_width // chips), (1, 2, 0, 3)
        ).reshape(rows, width)
        x_all = jnp.stack(slice_parts, axis=1).reshape(-1, depth)
        g_all = jnp.stack(grads).reshape(-1, columns)
        dense = jnp.einsum("tk,tn->kn", x_all, g_all, preferred_element_type=F32) * grad_scale
        dense = jnp.transpose(
            dense.reshape(row_tiles, 2, tile_rows, col_tiles, tile_width), (1, 0, 3, 2, 4)
        ).reshape(2, row_tiles * col_tiles, tile_rows, tile_width)
        picked = jnp.take(dense, tile_row[0] * col_tiles + tile_col[0], axis=1)
        mine = jnp.where(core == 0, picked[0], picked[1])
        theirs = jnp.where(core == 0, picked[1], picked[0])
        grad_tiles = mine + to_core(theirs)
    grad_tiles = jnp.transpose(grad_tiles, (1, 0, 2))
    return (act, grad_tokens, grad_tiles)


def solution(mesh):
    in_specs = (
        P(("fsdp", "tp"), None),
        P("fsdp", "tp", None),
        P("tp", None),
        P("tp", None),
        P("fsdp", "tp"),
    )
    out_specs = (P("fsdp", "tp"), P(("fsdp", "tp"), None), P("fsdp", "tp", None))
    return jax.shard_map(local, mesh=mesh, in_specs=in_specs, out_specs=out_specs, check_vma=False)
```

```python
import functools
import math

import jax
import jax.numpy as jnp
from jax import lax
from jax.experimental import pallas as pl
from jax.experimental.pallas import tpu as pltpu
from jax.sharding import PartitionSpec as P

SQRT_TWO_PI = 0.7978845608028654
CUBIC_COEF = 0.044715
BF16 = jnp.bfloat16
F32 = jnp.float32
VMEM = pltpu.VMEM
SMEM = pltpu.SMEM
MIB = 1 << 20


def gelu_pair(pre_act):
    gelu_inner = SQRT_TWO_PI * (pre_act + CUBIC_COEF * pre_act * pre_act * pre_act)
    tanh_inner = jnp.tanh(gelu_inner)
    act_value = 0.5 * pre_act * (1.0 + tanh_inner)
    act_slope = 0.5 * (1.0 + tanh_inner) + 0.5 * pre_act * (
        1.0 - tanh_inner * tanh_inner
    ) * SQRT_TWO_PI * (1.0 + 3.0 * CUBIC_COEF * pre_act * pre_act)
    return (act_value, act_slope)


def spec(space=VMEM):
    return pl.BlockSpec(memory_space=space)


def lane_regroup(chips, tile_width):
    size = chips * tile_width
    part = tile_width // chips
    column = lax.broadcasted_iota(jnp.int32, (1, size), 1)
    chip = column // tile_width
    inner = column % tile_width
    source = (inner // part) * tile_width + chip * part + inner % part
    row = lax.broadcasted_iota(jnp.int32, (size, size), 0)
    return jnp.where(row == source, 1.0, 0.0).astype(BF16)


def split_kernel(parts, tile_width, place_ref, tokens_ref, out_ref, onehot_ref):
    size = parts * tile_width
    rows = tokens_ref.shape[0]
    onehot_ref[...] = lane_regroup(parts, tile_width)
    me = place_ref[0]
    groups = tokens_ref.shape[1] // size
    lanes = jnp.concatenate(
        [tokens_ref[:, group * size : (group + 1) * size] for group in range(groups)], axis=0
    )
    picked = jnp.dot(lanes, onehot_ref[...], preferred_element_type=F32).astype(BF16)
    for part in range(parts):
        for group in range(groups):
            out_ref[me ^ part, :, group * tile_width : (group + 1) * tile_width] = picked[
                group * rows : (group + 1) * rows, part * tile_width : (part + 1) * tile_width
            ]


def join_kernel(parts, tile_width, place_ref, onehot_ref, *refs):
    *part_refs, out_ref, held = refs
    size = parts * tile_width
    rows = out_ref.shape[0]
    me = place_ref[0]
    groups = out_ref.shape[1] // size
    for step in range(parts // 2):
        total = part_refs[0][step]
        for part_ref in part_refs[1:]:
            total = total + part_ref[step].astype(F32)
        total = total.astype(BF16)
        for half in range(2):
            for group in range(groups):
                at = (half * groups + group) * tile_width
                held[me ^ (2 * step + half), group * rows : (group + 1) * rows] = total[
                    :, at : at + tile_width
                ]
    lanes = jnp.concatenate([held[part] for part in range(parts)], axis=1)
    result = jnp.dot(lanes, onehot_ref[...], preferred_element_type=F32).astype(BF16)
    for group in range(groups):
        out_ref[:, group * size : (group + 1) * size] = result[group * rows : (group + 1) * rows]


def place_tiles(half, row_ref, col_ref, tiles_ref, out_ref, first=0, count=None):
    slots, rows, width = tiles_ref.shape
    slots = slots if count is None else count
    start = half * (out_ref.shape[0] // 2)

    def place(slot, carry):
        top = pl.multiple_of(row_ref[0, first + slot] * rows + start, rows)
        left = pl.multiple_of(col_ref[0, first + slot] * width, width)
        out_ref[pl.ds(top, rows), pl.ds(left, width)] = tiles_ref[slot]
        return carry

    lax.fori_loop(0, slots, place, 0, unroll=35)


def weight_kernel(order_ref, row_ref, col_ref, own_ref, other_ref, w_ref):
    w_ref[...] = jnp.zeros_like(w_ref)
    place_tiles(0, row_ref, col_ref, own_ref, w_ref)
    place_tiles(1, row_ref, col_ref, other_ref, w_ref)


def early_kernel(n_tp, step, w_ref, *refs):
    x_refs = refs[:n_tp]
    *early_refs, sum_ref = refs[n_tp:]
    product = jnp.dot(slice_rows(x_refs, step), w_ref[...], preferred_element_type=F32)
    sum_ref[...] = product + early_refs[0][...] if early_refs else product


def relay_kernel(first_ref, second_ref, lower_ref, upper_ref):
    lower_ref[...] = first_ref[: lower_ref.shape[0]]
    upper_ref[...] = second_ref[lower_ref.shape[0] :]


def blank_kernel(order_ref, out_ref):
    out_ref[...] = jnp.zeros_like(out_ref)


def half_weight_kernel(n_tp, step, half, order_ref, row_ref, col_ref, lower_ref, upper_ref, blank_ref, early_ref, *refs):
    x_refs = refs[:n_tp]
    out_ref, sum_ref = refs[n_tp:]
    slots = row_ref.shape[1]
    rows = out_ref.shape[0] // 2
    place_tiles(0, row_ref, col_ref, lower_ref, out_ref, 0, half)
    place_tiles(0, row_ref, col_ref, upper_ref, out_ref, half, slots - half)
    lhs = jnp.concatenate([x_ref[2 * step] for x_ref in x_refs], axis=0)
    sum_ref[...] = early_ref[...] + jnp.dot(
        lhs, out_ref[:rows, :], preferred_element_type=F32
    )


def slice_rows(x_refs, step):
    return jnp.concatenate(
        [jnp.concatenate([x_ref[2 * step], x_ref[2 * step + 1]], axis=1) for x_ref in x_refs],
        axis=0,
    )


def hidden_kernel(n_tp, step, half, order_ref, z_ref, row_ref, col_ref, lower_ref, upper_ref, early_ref, cotangent_ref, half_ref, *refs):
    x_refs = refs[:n_tp]
    w_ref, act_ref, grad_ref, *pack_refs = refs[n_tp:]
    rows = x_refs[0].shape[1]
    place_tiles(1, row_ref, col_ref, lower_ref, w_ref, 0, half)
    place_tiles(1, row_ref, col_ref, upper_ref, w_ref, half, row_ref.shape[1] - half)
    half_rows = w_ref.shape[0] // 2
    lhs = jnp.concatenate([x_ref[2 * step + 1] for x_ref in x_refs], axis=0)
    for left, right in column_blocks(w_ref.shape[1]):
        hidden = early_ref[:, left:right] + jnp.dot(
            lhs, w_ref[half_rows:, left:right], preferred_element_type=F32
        )
        act_value, act_slope = gelu_pair(hidden)
        act_value = act_value.astype(BF16)
        for j in range(n_tp):
            at = pl.ds(pl.multiple_of((z_ref[0] ^ j) * rows, rows), rows)
            act_ref[at, left:right] = act_value[j * rows : (j + 1) * rows]
            slope = act_slope[j * rows : (j + 1) * rows]
            grad = (cotangent_ref[at, left:right].astype(F32) * slope).astype(BF16)
            for out_ref in (grad_ref, *pack_refs):
                out_ref[j * rows : (j + 1) * rows, left:right] = grad
    for chip, pack_ref in enumerate(pack_refs):
        pack_ref[:, w_ref.shape[1] :] = slice_rows(x_refs, chip)


def column_blocks(columns, block=512):
    return [(left, min(left + block, columns)) for left in range(0, columns, block)]


def back_kernel(n_tp, first, count, g_ref, *refs):
    w_refs = refs[:count]
    out_refs = refs[-n_tp:]
    rows = g_ref.shape[0] // n_tp
    for step in range(count):
        result = lax.dot_general(
            w_refs[step][...], g_ref[...], (((1,), (1,)), ((), ())), preferred_element_type=F32
        ).T
        for j in range(n_tp):
            out_refs[j][first + step] = result[j * rows : (j + 1) * rows].astype(out_refs[j].dtype)


def tile_grad_kernel(chips, scale, order_ref, row_ref, col_ref, *refs):
    pack_refs = refs[:chips]
    mine_ref, theirs_ref, dense = refs[chips:]
    slots, tile_rows, width = mine_ref.shape
    columns = dense.shape[1]
    half = dense.shape[0] // 2
    x_t = jnp.concatenate([pack_ref[:, columns:] for pack_ref in pack_refs], axis=0).T
    for left, right in column_blocks(columns):
        g_all = jnp.concatenate([pack_ref[:, left:right] for pack_ref in pack_refs], axis=0)
        dense[:, left:right] = jnp.dot(x_t, g_all, preferred_element_type=F32)

    def place_tile(slot, carry):
        top = pl.multiple_of(row_ref[0, slot] * tile_rows, tile_rows)
        left = pl.multiple_of(col_ref[0, slot] * width, width)
        low = pl.multiple_of(top + half, tile_rows)
        mine_ref[slot] = dense[pl.ds(top, tile_rows), pl.ds(left, width)] * scale
        theirs_ref[slot] = (dense[pl.ds(low, tile_rows), pl.ds(left, width)] * scale).astype(
            theirs_ref.dtype
        )
        return carry

    lax.fori_loop(0, slots, place_tile, 0, unroll=35)


def params(limit):
    return pltpu.CompilerParams(vmem_limit_bytes=limit * MIB)


def cost(flops, bytes_accessed):
    return pl.CostEstimate(flops=flops >> 12, bytes_accessed=bytes_accessed >> 12, transcendentals=0)


def local(tokens, tile_values, tile_row, tile_col, grad_act):
    fsdp = lax.axis_size("fsdp")
    n_tp = lax.axis_size("tp")
    chips = fsdp // 2
    rows, width = tokens.shape
    tile_rows, slots, tile_width = tile_values.shape
    row_tiles = width // tile_width
    columns = grad_act.shape[1]
    col_tiles = columns // tile_width
    depth = row_tiles * 2 * tile_rows
    total_tokens = rows * fsdp * n_tp
    grad_scale = 1.0 / math.sqrt(total_tokens)
    place = lax.axis_index("fsdp")
    chip = place // 2
    core = place % 2
    z = lax.axis_index("tp")
    paired = n_tp & (n_tp - 1) == 0
    fast = (
        tile_rows % 16 == 0 and rows % 16 == 0 and row_tiles % fsdp == 0 and n_tp == 4 and chips == 4
    )

    def to_core(value):
        return lax.ppermute(value, "fsdp", [(f, f ^ 1) for f in range(fsdp)])

    def to_chip(value, step):
        return lax.ppermute(value, "fsdp", [(f, f ^ (2 * step)) for f in range(fsdp)])

    def to_z(value, step):
        if paired:
            return lax.ppermute(value, "tp", [(i, i ^ step) for i in range(n_tp)])
        return lax.ppermute(value, "tp", [(i, (i + step) % n_tp) for i in range(n_tp)])

    def from_z(value, step):
        return to_z(value, step if paired else n_tp - step)

    def z_rows(step):
        return (z ^ step if paired else (z - step) % n_tp) * rows

    def after(value, *earlier):
        return lax.optimization_barrier((value, *earlier))[0]

    def along_z(value):
        parts = [value]
        for j in range(1, n_tp):
            parts.append(to_z(parts[2], 1) if paired and j == 3 else to_z(value, j))
        return parts

    z_index = z.astype(jnp.int32).reshape(1)

    place_index = place.astype(jnp.int32).reshape(1)
    tiles = [jnp.transpose(tile_values, (1, 0, 2))]
    block = rows * n_tp
    if fast:
        def make_weight(step, order):
            return pl.pallas_call(
                weight_kernel,
                out_shape=jax.ShapeDtypeStruct((depth, columns), BF16),
                in_specs=[spec(SMEM)] * 3 + [spec()] * 2,
                out_specs=spec(),
                compiler_params=params(10),
                cost_estimate=cost(0, 2 * 2 * depth * columns),
            )(order, tile_row, tile_col, tiles[step], others[step])

        def add_hidden(step, *early):
            return pl.pallas_call(
                functools.partial(early_kernel, n_tp, step),
                out_shape=jax.ShapeDtypeStruct((block, columns), F32),
                in_specs=[spec()] * (1 + n_tp + len(early)),
                out_specs=spec(),
                compiler_params=params(14),
                cost_estimate=cost(2 * block * depth * columns, 2 * depth * columns),
            )(weights[step], *token_parts, *early)

        others = [to_core(tiles[0])]
        split, onehot = pl.pallas_call(
            functools.partial(split_kernel, fsdp, tile_width),
            out_shape=[
                jax.ShapeDtypeStruct((fsdp, rows, depth // 2), BF16),
                jax.ShapeDtypeStruct((fsdp * tile_width, fsdp * tile_width), BF16),
            ],
            in_specs=[spec(SMEM), spec()],
            out_specs=[spec()] * 2,
            compiler_params=params(8),
        )(place_index, tokens)
        token_parts = along_z(split)
        tiles += [to_chip(tiles[0], 1), to_chip(tiles[0], 2)]
        weights = [make_weight(0, z_index)]
        blank = pl.pallas_call(
            blank_kernel,
            out_shape=jax.ShapeDtypeStruct((depth, columns), BF16),
            in_specs=[spec(SMEM)],
            out_specs=spec(),
            compiler_params=params(10),
            cost_estimate=cost(0, 2 * depth * columns),
        )(after(z_index, token_parts[2]))
        tiles[1], tiles[2], blank, *_ = lax.optimization_barrier(
            (tiles[1], tiles[2], blank, *token_parts[1:], weights[0])
        )
        half = slots // 2
        relay = pl.pallas_call(
            relay_kernel,
            out_shape=[
                jax.ShapeDtypeStruct((half, tile_rows, tile_width), BF16),
                jax.ShapeDtypeStruct((slots - half, tile_rows, tile_width), BF16),
            ],
            in_specs=[spec()] * 2,
            out_specs=[spec()] * 2,
            compiler_params=params(8),
        )(tiles[1], tiles[2])
        relayed = [to_chip(relay[0], 2), to_chip(relay[1], 1)]
        others += [to_core(after(part, *relay)) for part in tiles[1:]]
        for step in range(1, chips - 1):
            weights.append(make_weight(step, after(z_index, weights[-1], *relay)))
        early = add_hidden(0)
        for step in range(1, chips - 1):
            early = add_hidden(step, early)
        *relayed, _ = lax.optimization_barrier((*relayed, early))
        last_others = [to_core(part) for part in relayed]
    else:
        tiles += [to_chip(tiles[0], step) for step in range(1, chips)]
        others = [to_core(part) for part in tiles]
        split = jnp.transpose(
            tokens.reshape(rows, row_tiles, chips, tile_width // chips), (2, 0, 1, 3)
        ).reshape(chips, rows, depth)
        split = jnp.take(split, jnp.arange(chips) ^ chip, axis=0)
        token_parts = along_z(split)
        pieces = [split[0]] + [to_chip(split[step], step) for step in range(1, chips)]
        slice_parts = along_z(jnp.stack(pieces))

    if fast:
        half_weight, early = pl.pallas_call(
            functools.partial(half_weight_kernel, n_tp, chips - 1, half),
            out_shape=[
                jax.ShapeDtypeStruct((depth, columns), BF16),
                jax.ShapeDtypeStruct((block, columns), F32),
            ],
            in_specs=[spec(SMEM)] * 3 + [spec()] * (4 + n_tp),
            out_specs=[spec()] * 2,
            input_output_aliases={5: 0, 6: 1},
            compiler_params=params(20),
            cost_estimate=cost(block * depth * columns, 2 * depth * columns),
        )(z_index, tile_row, tile_col, *relayed, blank, early, *token_parts)
        last_weight, act, hidden_grad, *packs = pl.pallas_call(
            functools.partial(hidden_kernel, n_tp, chips - 1, half),
            out_shape=[
                jax.ShapeDtypeStruct((depth, columns), BF16),
                jax.ShapeDtypeStruct((block, columns), BF16),
                jax.ShapeDtypeStruct((block, columns), BF16),
            ]
            + [jax.ShapeDtypeStruct((block, columns + depth), BF16)] * chips,
            in_specs=[spec(SMEM)] * 4 + [spec()] * (5 + n_tp),
            out_specs=[spec()] * (3 + chips),
            input_output_aliases={8: 0},
            compiler_params=params(24),
            cost_estimate=cost(2 * block * depth * columns, 2 * depth * columns),
        )(
            z_index, z_index, tile_row, tile_col, *last_others, early, grad_act, half_weight,
            *token_parts,
        )
        weights.append(last_weight)
    else:
        mine = jnp.stack(tiles, axis=1)
        theirs = jnp.stack(others, axis=1)
        both = jnp.where(
            core == 0,
            jnp.concatenate([mine, theirs], axis=2),
            jnp.concatenate([theirs, mine], axis=2),
        )
        flat = tile_row[0] * col_tiles + tile_col[0]
        weight = jnp.zeros((row_tiles * col_tiles, chips, 2 * tile_rows, tile_width), BF16)
        weight = weight.at[flat].set(both, unique_indices=True)
        weight = jnp.transpose(
            weight.reshape(row_tiles, col_tiles, chips, 2 * tile_rows, tile_width),
            (2, 0, 3, 1, 4),
        ).reshape(chips, depth, columns)
        hidden = jnp.einsum(
            "jqrk,qkc->jrc", jnp.stack(token_parts), weight, preferred_element_type=F32
        )
        act_value, act_slope = gelu_pair(hidden)
        act_value = act_value.astype(BF16)
        cotangent = jnp.stack(
            [lax.dynamic_slice_in_dim(grad_act, z_rows(j), rows, axis=0) for j in range(n_tp)]
        )
        hidden_grad = (cotangent.astype(F32) * act_slope).astype(BF16).reshape(block, columns)
        act = jnp.zeros((block, columns), BF16)
        for j in range(n_tp):
            act = lax.dynamic_update_slice_in_dim(act, act_value[j], z_rows(j), axis=0)


    if fast:
        packs = [packs[0]] + [to_chip(packs[step], step) for step in range(1, chips)]
        backs = []
        for first in range(0, chips, 2):
            backs = pl.pallas_call(
                functools.partial(back_kernel, n_tp, first, 2),
                out_shape=[
                    jax.ShapeDtypeStruct((chips, rows, depth), F32 if j == 0 else BF16)
                    for j in range(n_tp)
                ],
                in_specs=[spec()] * (3 + len(backs)),
                out_specs=[spec()] * n_tp,
                input_output_aliases={3 + j: j for j in range(n_tp)} if backs else {},
                compiler_params=params(18),
                cost_estimate=cost(4 * block * depth * columns, 4 * depth * columns),
            )(hidden_grad, *weights[first : first + 2], *backs)
        near = after(backs[1], packs[1])
        returned = [backs[0]] + [
            to_z(near if j == 1 else backs[j], j) for j in range(1, n_tp)
        ]
        mine, theirs = pl.pallas_call(
            functools.partial(tile_grad_kernel, chips, grad_scale),
            out_shape=[
                jax.ShapeDtypeStruct((slots, tile_rows, tile_width), F32),
                jax.ShapeDtypeStruct((slots, tile_rows, tile_width), BF16),
            ],
            in_specs=[spec(SMEM)] * 3 + [spec()] * chips,
            out_specs=[spec()] * 2,
            scratch_shapes=[pltpu.VMEM((depth, columns), F32)],
            compiler_params=params(28),
            cost_estimate=cost(2 * chips * block * depth * columns, 4 * depth * columns),
        )(after(z_index, *returned[1:]), tile_row, tile_col, *packs)
        grad_tiles = mine + to_core(theirs).astype(F32)
        grad_tokens = pl.pallas_call(
            functools.partial(join_kernel, fsdp, tile_width),
            out_shape=jax.ShapeDtypeStruct((rows, width), BF16),
            in_specs=[spec(SMEM)] + [spec()] * (1 + n_tp),
            out_specs=spec(),
            scratch_shapes=[pltpu.VMEM((fsdp, rows * row_tiles // fsdp, tile_width), BF16)],
            compiler_params=params(8),
        )(place_index, onehot, *returned)
    else:
        grads = [hidden_grad] + [to_chip(hidden_grad, step) for step in range(1, chips)]
        backs = jnp.einsum(
            "jrc,qkc->jqrk",
            hidden_grad.reshape(n_tp, rows, columns),
            weight,
            preferred_element_type=F32,
        )
        total = backs[0]
        for j in range(1, n_tp):
            total = total + from_z(backs[j].astype(BF16), j).astype(F32)
        joined = jnp.take(total.astype(BF16), jnp.arange(chips) ^ chip, axis=0)
        grad_tokens = jnp.transpose(
            joined.reshape(chips, rows, row_tiles, tile_width // chips), (1, 2, 0, 3)
        ).reshape(rows, width)
        x_all = jnp.stack(slice_parts, axis=1).reshape(-1, depth)
        g_all = jnp.stack(grads).reshape(-1, columns)
        dense = jnp.einsum("tk,tn->kn", x_all, g_all, preferred_element_type=F32) * grad_scale
        dense = jnp.transpose(
            dense.reshape(row_tiles, 2, tile_rows, col_tiles, tile_width), (1, 0, 3, 2, 4)
        ).reshape(2, row_tiles * col_tiles, tile_rows, tile_width)
        picked = jnp.take(dense, tile_row[0] * col_tiles + tile_col[0], axis=1)
        mine = jnp.where(core == 0, picked[0], picked[1])
        theirs = jnp.where(core == 0, picked[1], picked[0])
        grad_tiles = mine + to_core(theirs)
    grad_tiles = jnp.transpose(grad_tiles, (1, 0, 2))
    return (act, grad_tokens, grad_tiles)


def solution(mesh):
    in_specs = (
        P(("fsdp", "tp"), None),
        P("fsdp", "tp", None),
        P("tp", None),
        P("tp", None),
        P("fsdp", "tp"),
    )
    out_specs = (P("fsdp", "tp"), P(("fsdp", "tp"), None), P("fsdp", "tp", None))
    return jax.shard_map(local, mesh=mesh, in_specs=in_specs, out_specs=out_specs, check_vma=False)
```

```python
import functools
import math

import jax
import jax.numpy as jnp
from jax import lax
from jax.experimental import pallas as pl
from jax.experimental.pallas import tpu as pltpu
from jax.sharding import PartitionSpec as P

SQRT_TWO_PI = 0.7978845608028654
CUBIC_COEF = 0.044715
BF16 = jnp.bfloat16
F32 = jnp.float32
VMEM = pltpu.VMEM
SMEM = pltpu.SMEM
MIB = 1 << 20


def gelu_pair(pre_act):
    gelu_inner = SQRT_TWO_PI * (pre_act + CUBIC_COEF * pre_act * pre_act * pre_act)
    tanh_inner = jnp.tanh(gelu_inner)
    act_value = 0.5 * pre_act * (1.0 + tanh_inner)
    act_slope = 0.5 * (1.0 + tanh_inner) + 0.5 * pre_act * (
        1.0 - tanh_inner * tanh_inner
    ) * SQRT_TWO_PI * (1.0 + 3.0 * CUBIC_COEF * pre_act * pre_act)
    return (act_value, act_slope)


def spec(space=VMEM):
    return pl.BlockSpec(memory_space=space)


def lane_regroup(chips, tile_width):
    size = chips * tile_width
    part = tile_width // chips
    column = lax.broadcasted_iota(jnp.int32, (1, size), 1)
    chip = column // tile_width
    inner = column % tile_width
    source = (inner // part) * tile_width + chip * part + inner % part
    row = lax.broadcasted_iota(jnp.int32, (size, size), 0)
    return jnp.where(row == source, 1.0, 0.0).astype(BF16)


def split_kernel(parts, tile_width, place_ref, tokens_ref, out_ref, onehot_ref):
    size = parts * tile_width
    rows = tokens_ref.shape[0]
    onehot_ref[...] = lane_regroup(parts, tile_width)
    me = place_ref[0]
    groups = tokens_ref.shape[1] // size
    lanes = jnp.concatenate(
        [tokens_ref[:, group * size : (group + 1) * size] for group in range(groups)], axis=0
    )
    picked = jnp.dot(lanes, onehot_ref[...], preferred_element_type=F32).astype(BF16)
    for part in range(parts):
        for group in range(groups):
            out_ref[me ^ part, :, group * tile_width : (group + 1) * tile_width] = picked[
                group * rows : (group + 1) * rows, part * tile_width : (part + 1) * tile_width
            ]


def join_kernel(parts, tile_width, place_ref, onehot_ref, *refs):
    *part_refs, out_ref, held = refs
    size = parts * tile_width
    rows = out_ref.shape[0]
    me = place_ref[0]
    groups = out_ref.shape[1] // size
    for step in range(parts // 2):
        total = part_refs[0][step]
        for part_ref in part_refs[1:]:
            total = total + part_ref[step].astype(F32)
        total = total.astype(BF16)
        for half in range(2):
            for group in range(groups):
                at = (half * groups + group) * tile_width
                held[me ^ (2 * step + half), group * rows : (group + 1) * rows] = total[
                    :, at : at + tile_width
                ]
    lanes = jnp.concatenate([held[part] for part in range(parts)], axis=1)
    result = jnp.dot(lanes, onehot_ref[...], preferred_element_type=F32).astype(BF16)
    for group in range(groups):
        out_ref[:, group * size : (group + 1) * size] = result[group * rows : (group + 1) * rows]


def place_tiles(half, row_ref, col_ref, tiles_ref, out_ref, first=0, count=None):
    slots, rows, width = tiles_ref.shape
    slots = slots if count is None else count
    start = half * (out_ref.shape[0] // 2)

    def place(slot, carry):
        top = pl.multiple_of(row_ref[0, first + slot] * rows + start, rows)
        left = pl.multiple_of(col_ref[0, first + slot] * width, width)
        out_ref[pl.ds(top, rows), pl.ds(left, width)] = tiles_ref[slot]
        return carry

    lax.fori_loop(0, slots, place, 0, unroll=35)


def weight_kernel(order_ref, row_ref, col_ref, own_ref, other_ref, w_ref):
    w_ref[...] = jnp.zeros_like(w_ref)
    place_tiles(0, row_ref, col_ref, own_ref, w_ref)
    place_tiles(1, row_ref, col_ref, other_ref, w_ref)


def early_kernel(n_tp, step, w_ref, *refs):
    x_refs = refs[:n_tp]
    *early_refs, sum_ref = refs[n_tp:]
    product = jnp.dot(slice_rows(x_refs, step), w_ref[...], preferred_element_type=F32)
    sum_ref[...] = product + early_refs[0][...] if early_refs else product


def relay_kernel(first_ref, second_ref, lower_ref, upper_ref):
    lower_ref[...] = first_ref[: lower_ref.shape[0]]
    upper_ref[...] = second_ref[lower_ref.shape[0] :]


def blank_kernel(order_ref, out_ref):
    out_ref[...] = jnp.zeros_like(out_ref)


def half_weight_kernel(n_tp, step, half, order_ref, row_ref, col_ref, lower_ref, upper_ref, blank_ref, early_ref, *refs):
    x_refs = refs[:n_tp]
    out_ref, sum_ref = refs[n_tp:]
    slots = row_ref.shape[1]
    rows = out_ref.shape[0] // 2
    place_tiles(0, row_ref, col_ref, lower_ref, out_ref, 0, half)
    place_tiles(0, row_ref, col_ref, upper_ref, out_ref, half, slots - half)
    lhs = jnp.concatenate([x_ref[2 * step] for x_ref in x_refs], axis=0)
    sum_ref[...] = early_ref[...] + jnp.dot(
        lhs, out_ref[:rows, :], preferred_element_type=F32
    )


def slice_rows(x_refs, step):
    return jnp.concatenate(
        [jnp.concatenate([x_ref[2 * step], x_ref[2 * step + 1]], axis=1) for x_ref in x_refs],
        axis=0,
    )


def hidden_kernel(n_tp, step, half, order_ref, z_ref, row_ref, col_ref, lower_ref, upper_ref, early_ref, cotangent_ref, half_ref, *refs):
    x_refs = refs[:n_tp]
    w_ref, act_ref, grad_ref, *pack_refs = refs[n_tp:]
    rows = x_refs[0].shape[1]
    place_tiles(1, row_ref, col_ref, lower_ref, w_ref, 0, half)
    place_tiles(1, row_ref, col_ref, upper_ref, w_ref, half, row_ref.shape[1] - half)
    half_rows = w_ref.shape[0] // 2
    lhs = jnp.concatenate([x_ref[2 * step + 1] for x_ref in x_refs], axis=0)
    for left, right in column_blocks(w_ref.shape[1]):
        hidden = early_ref[:, left:right] + jnp.dot(
            lhs, w_ref[half_rows:, left:right], preferred_element_type=F32
        )
        act_value, act_slope = gelu_pair(hidden)
        act_value = act_value.astype(BF16)
        for j in range(n_tp):
            at = pl.ds(pl.multiple_of((z_ref[0] ^ j) * rows, rows), rows)
            act_ref[at, left:right] = act_value[j * rows : (j + 1) * rows]
            slope = act_slope[j * rows : (j + 1) * rows]
            grad = (cotangent_ref[at, left:right].astype(F32) * slope).astype(BF16)
            for out_ref in (grad_ref, *pack_refs):
                out_ref[j * rows : (j + 1) * rows, left:right] = grad
    for chip, pack_ref in enumerate(pack_refs):
        pack_ref[:, w_ref.shape[1] :] = slice_rows(x_refs, chip)


def column_blocks(columns, block=896):
    return [(left, min(left + block, columns)) for left in range(0, columns, block)]


def back_kernel(n_tp, first, count, g_ref, *refs):
    w_refs = refs[:count]
    out_refs = refs[-n_tp:]
    rows = g_ref.shape[0] // n_tp
    for step in range(count):
        result = lax.dot_general(
            w_refs[step][...], g_ref[...], (((1,), (1,)), ((), ())), preferred_element_type=F32
        ).T
        for j in range(n_tp):
            out_refs[j][first + step] = result[j * rows : (j + 1) * rows].astype(out_refs[j].dtype)


def tile_grad_kernel(chips, scale, order_ref, row_ref, col_ref, *refs):
    pack_refs = refs[:chips]
    mine_ref, theirs_ref, dense = refs[chips:]
    slots, tile_rows, width = mine_ref.shape
    columns = dense.shape[1]
    half = dense.shape[0] // 2
    x_t = jnp.concatenate([pack_ref[:, columns:] for pack_ref in pack_refs], axis=0).T
    for left, right in column_blocks(columns):
        g_all = jnp.concatenate([pack_ref[:, left:right] for pack_ref in pack_refs], axis=0)
        dense[:, left:right] = jnp.dot(x_t, g_all, preferred_element_type=F32)

    def place_tile(slot, carry):
        top = pl.multiple_of(row_ref[0, slot] * tile_rows, tile_rows)
        left = pl.multiple_of(col_ref[0, slot] * width, width)
        low = pl.multiple_of(top + half, tile_rows)
        mine_ref[slot] = dense[pl.ds(top, tile_rows), pl.ds(left, width)] * scale
        theirs_ref[slot] = (dense[pl.ds(low, tile_rows), pl.ds(left, width)] * scale).astype(
            theirs_ref.dtype
        )
        return carry

    lax.fori_loop(0, slots, place_tile, 0, unroll=35)


def params(limit):
    return pltpu.CompilerParams(vmem_limit_bytes=limit * MIB)


def cost(flops, bytes_accessed):
    return pl.CostEstimate(flops=flops >> 12, bytes_accessed=bytes_accessed >> 12, transcendentals=0)


def local(tokens, tile_values, tile_row, tile_col, grad_act):
    fsdp = lax.axis_size("fsdp")
    n_tp = lax.axis_size("tp")
    chips = fsdp // 2
    rows, width = tokens.shape
    tile_rows, slots, tile_width = tile_values.shape
    row_tiles = width // tile_width
    columns = grad_act.shape[1]
    col_tiles = columns // tile_width
    depth = row_tiles * 2 * tile_rows
    total_tokens = rows * fsdp * n_tp
    grad_scale = 1.0 / math.sqrt(total_tokens)
    place = lax.axis_index("fsdp")
    chip = place // 2
    core = place % 2
    z = lax.axis_index("tp")
    paired = n_tp & (n_tp - 1) == 0
    fast = (
        tile_rows % 16 == 0 and rows % 16 == 0 and row_tiles % fsdp == 0 and n_tp == 4 and chips == 4
    )

    def to_core(value):
        return lax.ppermute(value, "fsdp", [(f, f ^ 1) for f in range(fsdp)])

    def to_chip(value, step):
        return lax.ppermute(value, "fsdp", [(f, f ^ (2 * step)) for f in range(fsdp)])

    def to_z(value, step):
        if paired:
            return lax.ppermute(value, "tp", [(i, i ^ step) for i in range(n_tp)])
        return lax.ppermute(value, "tp", [(i, (i + step) % n_tp) for i in range(n_tp)])

    def from_z(value, step):
        return to_z(value, step if paired else n_tp - step)

    def z_rows(step):
        return (z ^ step if paired else (z - step) % n_tp) * rows

    def after(value, *earlier):
        return lax.optimization_barrier((value, *earlier))[0]

    def along_z(value):
        parts = [value]
        for j in range(1, n_tp):
            parts.append(to_z(parts[2], 1) if paired and j == 3 else to_z(value, j))
        return parts

    z_index = z.astype(jnp.int32).reshape(1)

    place_index = place.astype(jnp.int32).reshape(1)
    tiles = [jnp.transpose(tile_values, (1, 0, 2))]
    block = rows * n_tp
    if fast:
        def make_weight(step, order):
            return pl.pallas_call(
                weight_kernel,
                out_shape=jax.ShapeDtypeStruct((depth, columns), BF16),
                in_specs=[spec(SMEM)] * 3 + [spec()] * 2,
                out_specs=spec(),
                compiler_params=params(10),
                cost_estimate=cost(0, 2 * 2 * depth * columns),
            )(order, tile_row, tile_col, tiles[step], others[step])

        def add_hidden(step, *early):
            return pl.pallas_call(
                functools.partial(early_kernel, n_tp, step),
                out_shape=jax.ShapeDtypeStruct((block, columns), F32),
                in_specs=[spec()] * (1 + n_tp + len(early)),
                out_specs=spec(),
                compiler_params=params(14),
                cost_estimate=cost(2 * block * depth * columns, 2 * depth * columns),
            )(weights[step], *token_parts, *early)

        others = [to_core(tiles[0])]
        split, onehot = pl.pallas_call(
            functools.partial(split_kernel, fsdp, tile_width),
            out_shape=[
                jax.ShapeDtypeStruct((fsdp, rows, depth // 2), BF16),
                jax.ShapeDtypeStruct((fsdp * tile_width, fsdp * tile_width), BF16),
            ],
            in_specs=[spec(SMEM), spec()],
            out_specs=[spec()] * 2,
            compiler_params=params(8),
        )(place_index, tokens)
        token_parts = along_z(split)
        tiles += [to_chip(tiles[0], 1), to_chip(tiles[0], 2)]
        weights = [make_weight(0, z_index)]
        blank = pl.pallas_call(
            blank_kernel,
            out_shape=jax.ShapeDtypeStruct((depth, columns), BF16),
            in_specs=[spec(SMEM)],
            out_specs=spec(),
            compiler_params=params(10),
            cost_estimate=cost(0, 2 * depth * columns),
        )(after(z_index, token_parts[2]))
        tiles[1], tiles[2], blank, *_ = lax.optimization_barrier(
            (tiles[1], tiles[2], blank, *token_parts[1:], weights[0])
        )
        half = slots // 2
        relay = pl.pallas_call(
            relay_kernel,
            out_shape=[
                jax.ShapeDtypeStruct((half, tile_rows, tile_width), BF16),
                jax.ShapeDtypeStruct((slots - half, tile_rows, tile_width), BF16),
            ],
            in_specs=[spec()] * 2,
            out_specs=[spec()] * 2,
            compiler_params=params(8),
        )(tiles[1], tiles[2])
        relayed = [to_chip(relay[0], 2), to_chip(relay[1], 1)]
        others += [to_core(after(part, *relay)) for part in tiles[1:]]
        for step in range(1, chips - 1):
            weights.append(make_weight(step, after(z_index, weights[-1], *relay)))
        early = add_hidden(0)
        for step in range(1, chips - 1):
            early = add_hidden(step, early)
        *relayed, _ = lax.optimization_barrier((*relayed, early))
        last_others = [to_core(part) for part in relayed]
    else:
        tiles += [to_chip(tiles[0], step) for step in range(1, chips)]
        others = [to_core(part) for part in tiles]
        split = jnp.transpose(
            tokens.reshape(rows, row_tiles, chips, tile_width // chips), (2, 0, 1, 3)
        ).reshape(chips, rows, depth)
        split = jnp.take(split, jnp.arange(chips) ^ chip, axis=0)
        token_parts = along_z(split)
        pieces = [split[0]] + [to_chip(split[step], step) for step in range(1, chips)]
        slice_parts = along_z(jnp.stack(pieces))

    if fast:
        half_weight, early = pl.pallas_call(
            functools.partial(half_weight_kernel, n_tp, chips - 1, half),
            out_shape=[
                jax.ShapeDtypeStruct((depth, columns), BF16),
                jax.ShapeDtypeStruct((block, columns), F32),
            ],
            in_specs=[spec(SMEM)] * 3 + [spec()] * (4 + n_tp),
            out_specs=[spec()] * 2,
            input_output_aliases={5: 0, 6: 1},
            compiler_params=params(20),
            cost_estimate=cost(block * depth * columns, 2 * depth * columns),
        )(z_index, tile_row, tile_col, *relayed, blank, early, *token_parts)
        last_weight, act, hidden_grad, *packs = pl.pallas_call(
            functools.partial(hidden_kernel, n_tp, chips - 1, half),
            out_shape=[
                jax.ShapeDtypeStruct((depth, columns), BF16),
                jax.ShapeDtypeStruct((block, columns), BF16),
                jax.ShapeDtypeStruct((block, columns), BF16),
            ]
            + [jax.ShapeDtypeStruct((block, columns + depth), BF16)] * chips,
            in_specs=[spec(SMEM)] * 4 + [spec()] * (5 + n_tp),
            out_specs=[spec()] * (3 + chips),
            input_output_aliases={8: 0},
            compiler_params=params(24),
            cost_estimate=cost(2 * block * depth * columns, 2 * depth * columns),
        )(
            z_index, z_index, tile_row, tile_col, *last_others, early, grad_act, half_weight,
            *token_parts,
        )
        weights.append(last_weight)
    else:
        mine = jnp.stack(tiles, axis=1)
        theirs = jnp.stack(others, axis=1)
        both = jnp.where(
            core == 0,
            jnp.concatenate([mine, theirs], axis=2),
            jnp.concatenate([theirs, mine], axis=2),
        )
        flat = tile_row[0] * col_tiles + tile_col[0]
        weight = jnp.zeros((row_tiles * col_tiles, chips, 2 * tile_rows, tile_width), BF16)
        weight = weight.at[flat].set(both, unique_indices=True)
        weight = jnp.transpose(
            weight.reshape(row_tiles, col_tiles, chips, 2 * tile_rows, tile_width),
            (2, 0, 3, 1, 4),
        ).reshape(chips, depth, columns)
        hidden = jnp.einsum(
            "jqrk,qkc->jrc", jnp.stack(token_parts), weight, preferred_element_type=F32
        )
        act_value, act_slope = gelu_pair(hidden)
        act_value = act_value.astype(BF16)
        cotangent = jnp.stack(
            [lax.dynamic_slice_in_dim(grad_act, z_rows(j), rows, axis=0) for j in range(n_tp)]
        )
        hidden_grad = (cotangent.astype(F32) * act_slope).astype(BF16).reshape(block, columns)
        act = jnp.zeros((block, columns), BF16)
        for j in range(n_tp):
            act = lax.dynamic_update_slice_in_dim(act, act_value[j], z_rows(j), axis=0)


    if fast:
        packs = [packs[0]] + [to_chip(packs[step], step) for step in range(1, chips)]
        backs = []
        for first in range(0, chips, 2):
            backs = pl.pallas_call(
                functools.partial(back_kernel, n_tp, first, 2),
                out_shape=[
                    jax.ShapeDtypeStruct((chips, rows, depth), F32 if j == 0 else BF16)
                    for j in range(n_tp)
                ],
                in_specs=[spec()] * (3 + len(backs)),
                out_specs=[spec()] * n_tp,
                input_output_aliases={3 + j: j for j in range(n_tp)} if backs else {},
                compiler_params=params(18),
                cost_estimate=cost(4 * block * depth * columns, 4 * depth * columns),
            )(hidden_grad, *weights[first : first + 2], *backs)
        near = after(backs[1], packs[1])
        returned = [backs[0]] + [
            to_z(near if j == 1 else backs[j], j) for j in range(1, n_tp)
        ]
        mine, theirs = pl.pallas_call(
            functools.partial(tile_grad_kernel, chips, grad_scale),
            out_shape=[
                jax.ShapeDtypeStruct((slots, tile_rows, tile_width), F32),
                jax.ShapeDtypeStruct((slots, tile_rows, tile_width), BF16),
            ],
            in_specs=[spec(SMEM)] * 3 + [spec()] * chips,
            out_specs=[spec()] * 2,
            scratch_shapes=[pltpu.VMEM((depth, columns), F32)],
            compiler_params=params(28),
            cost_estimate=cost(2 * chips * block * depth * columns, 4 * depth * columns),
        )(after(z_index, *returned[1:]), tile_row, tile_col, *packs)
        grad_tiles = mine + to_core(theirs).astype(F32)
        grad_tokens = pl.pallas_call(
            functools.partial(join_kernel, fsdp, tile_width),
            out_shape=jax.ShapeDtypeStruct((rows, width), BF16),
            in_specs=[spec(SMEM)] + [spec()] * (1 + n_tp),
            out_specs=spec(),
            scratch_shapes=[pltpu.VMEM((fsdp, rows * row_tiles // fsdp, tile_width), BF16)],
            compiler_params=params(8),
        )(place_index, onehot, *returned)
    else:
        grads = [hidden_grad] + [to_chip(hidden_grad, step) for step in range(1, chips)]
        backs = jnp.einsum(
            "jrc,qkc->jqrk",
            hidden_grad.reshape(n_tp, rows, columns),
            weight,
            preferred_element_type=F32,
        )
        total = backs[0]
        for j in range(1, n_tp):
            total = total + from_z(backs[j].astype(BF16), j).astype(F32)
        joined = jnp.take(total.astype(BF16), jnp.arange(chips) ^ chip, axis=0)
        grad_tokens = jnp.transpose(
            joined.reshape(chips, rows, row_tiles, tile_width // chips), (1, 2, 0, 3)
        ).reshape(rows, width)
        x_all = jnp.stack(slice_parts, axis=1).reshape(-1, depth)
        g_all = jnp.stack(grads).reshape(-1, columns)
        dense = jnp.einsum("tk,tn->kn", x_all, g_all, preferred_element_type=F32) * grad_scale
        dense = jnp.transpose(
            dense.reshape(row_tiles, 2, tile_rows, col_tiles, tile_width), (1, 0, 3, 2, 4)
        ).reshape(2, row_tiles * col_tiles, tile_rows, tile_width)
        picked = jnp.take(dense, tile_row[0] * col_tiles + tile_col[0], axis=1)
        mine = jnp.where(core == 0, picked[0], picked[1])
        theirs = jnp.where(core == 0, picked[1], picked[0])
        grad_tiles = mine + to_core(theirs)
    grad_tiles = jnp.transpose(grad_tiles, (1, 0, 2))
    return (act, grad_tokens, grad_tiles)


def solution(mesh):
    in_specs = (
        P(("fsdp", "tp"), None),
        P("fsdp", "tp", None),
        P("tp", None),
        P("tp", None),
        P("fsdp", "tp"),
    )
    out_specs = (P("fsdp", "tp"), P(("fsdp", "tp"), None), P("fsdp", "tp", None))
    return jax.shard_map(local, mesh=mesh, in_specs=in_specs, out_specs=out_specs, check_vma=False)
```
